512 devices in a mesh: node: 64 (over x, z, core), local: 8 (over y).
Axes of the slice: x: 4, y: 8, z: 8, core: 2. Of those that a mesh axis runs over, the one named last changes fastest.
Arguments:
- master_weight: bfloat16 [64, 128, 2048], P(None, 'node', 'local'), may hold values from -6 to 6
- first_moment: float32 [64, 128, 2048], P(None, 'node', 'local'), may hold values from -6 to 6
- second_moment: float32 [64, 128, 2048], P(None, 'node', 'local'), may hold values from 0.25 to 4
- features: bfloat16 [128, 8, 128, 128], P('node', 'local'), may hold values from -6 to 6
- grad_out: bfloat16 [128, 8, 128, 2048], P('node', 'local'), may hold values from -0.1875 to 0.1875
- old_place: int32 [80], replicated, may hold values from 0 to 127, as said below
- new_place: int32 [80], replicated, may hold values from 0 to 127, as said below
- old_owner: int32 [16], replicated, may hold values from 0 to 63
- new_owner: int32 [16], replicated, may hold values from 0 to 63
Outputs:
- slot_weight: bfloat16 [128, 128, 2048], P('node', None, 'local')
- slot_first: float32 [128, 128, 2048], P('node', None, 'local')
- slot_second: float32 [128, 128, 2048], P('node', None, 'local')
The draws below stay inside these ranges and needn't reach their ends.
Inputs may be any that keep to these rules, and one draw needn't show every extreme that they name: `old_place`: 80 distinct positions; position p belongs to node p // 2; in every draw some node has all 2 of its positions taken. `new_place`: 80 distinct positions; position p belongs to node p // 2; in every draw some node has all 2 of its positions taken.
All inputs are finite; a program needn't handle non-finite values.
Results may differ from the reference program's by a relative error of at most 0.0044.
Values may be sent and summed in bfloat16 or wider, within the bound.
A program may use at most 64 MiB of HBM per device.

```python
import math
import jax
import jax.numpy as jnp
from jax import lax

EXPERTS = 64
REDUNDANT = 16
FF = 2048
ROWS = 128
TOK = 128
SLOTS = 80
CAP = 2
POSITIONS = 128
N_NODE = 64
N_LOCAL = 8


def place_draw(key):
    node_key, rest_key, order_key = jax.random.split(key, 3)
    full_node = jax.random.randint(node_key, (), 0, N_NODE).astype(jnp.int32)
    others = jax.random.permutation(rest_key, POSITIONS - CAP).astype(jnp.int32)
    others = jnp.where(others >= full_node * CAP, others + CAP, others)
    chosen = jnp.concatenate([full_node * CAP + jnp.arange(CAP, dtype=jnp.int32), others[:SLOTS - CAP]])
    order = jax.random.permutation(order_key, SLOTS)
    return chosen[order].astype(jnp.int32)


def draw_old_place(key, part):
    key = jax.random.fold_in(key, 11)
    return place_draw(key)


def draw_new_place(key, part):
    key = jax.random.fold_in(key, 23)
    return place_draw(key)


def set_ends(entries, stream_key, smallest, top_value):
    spot = [jax.random.randint(jax.random.fold_in(stream_key, axis), (), 0, length) for axis, length in enumerate(entries.shape)]
    longest = entries.shape.index(max(entries.shape))
    beside = spot[:longest] + [(spot[longest] + 1) % entries.shape[longest]] + spot[longest + 1:]
    return entries.at[tuple(spot)].set(smallest).at[tuple(beside)].set(top_value)


def steps_of(key, dims, shards, low, high):
    gain, own = 1.0, jax.random.fold_in(key, 6)
    for axis_at, parts in shards:
        heights = jnp.exp(jax.random.uniform(jax.random.fold_in(own, axis_at), (parts,), jnp.float32, low / len(shards), high / len(shards)))
        gain = gain * jnp.repeat(heights, dims[axis_at] // parts).reshape([-1 if axis == axis_at else 1 for axis in range(len(dims))])
    return gain


def bell_draw(rng, dims, width, most, pieces=(), held_as=jnp.bfloat16):
    array = width * jax.random.normal(rng, dims, jnp.float32)
    if pieces:
        array = array * steps_of(rng, dims, pieces, -0.22, 0.18)
    return jnp.clip(array, -most, most).astype(held_as)


def setup_inputs(seed: int = 0) -> dict:
    key_list = jax.random.split(jax.random.key(seed), 10)
    master_weight = bell_draw(key_list[0], (EXPERTS, ROWS, FF), 1.0, 6.0, ((1, 64), (2, 8)))
    first_moment = bell_draw(key_list[1], (EXPERTS, ROWS, FF), 1.0, 6.0, ((1, 64), (2, 8)), jnp.float32)
    second_moment = jnp.clip(jnp.exp(math.log(4.0) - 2.7725887 * jax.random.uniform(key_list[2], (EXPERTS, ROWS, FF), jnp.float32) ** steps_of(key_list[2], (EXPERTS, ROWS, FF), ((1, 64), (2, 8)), -0.2, 0.2)), 0.25, 4.0)
    features = bell_draw(key_list[3], (POSITIONS, N_LOCAL, TOK, ROWS), 1.0, 6.0, ((0, 64), (1, 8)))
    grad_out = bell_draw(key_list[4], (POSITIONS, N_LOCAL, TOK, FF), (TOK * N_LOCAL) ** -0.5, 0.1875, ((0, 64), (1, 8)))
    old_place = draw_old_place(jax.random.fold_in(key_list[9], 71), 0)
    new_place = draw_new_place(jax.random.fold_in(key_list[9], 71), 0)
    old_owner = set_ends(jax.random.randint(key_list[7], (REDUNDANT,), 0, EXPERTS), jax.random.fold_in(key_list[7], 1), 0, EXPERTS - 1).astype(jnp.int32)
    new_owner = set_ends(jax.random.randint(key_list[8], (REDUNDANT,), 0, EXPERTS), jax.random.fold_in(key_list[8], 1), 0, EXPERTS - 1).astype(jnp.int32)
    return dict(master_weight=master_weight, first_moment=first_moment, second_moment=second_moment, features=features, grad_out=grad_out, old_place=old_place, new_place=new_place, old_owner=old_owner, new_owner=new_owner)


BETA_FIRST = 0.9
BETA_SECOND = 0.95
LEARNING_RATE = 0.1
DECAY_RATE = 0.1
EPSILON = 1e-08
CORRECT_FIRST = 1.0 - 0.9 ** 10
CORRECT_SECOND = 1.0 - 0.95 ** 10

def reference(master_weight, first_moment, second_moment, features, grad_out, old_place, new_place, old_owner, new_owner):
    primaries = jnp.arange(EXPERTS, dtype=jnp.int32)
    old_expert = jnp.concatenate([primaries, old_owner.astype(jnp.int32)])
    new_expert = jnp.concatenate([primaries, new_owner.astype(jnp.int32)])

    def slot_term(place):
        inputs = features[place].astype(jnp.float32)
        cotangent = grad_out[place].astype(jnp.float32)
        return jnp.einsum('ltr,ltf->rf', inputs, cotangent)
    slot_grad = lax.map(slot_term, old_place.astype(jnp.int32))
    gradient = jnp.zeros((EXPERTS, ROWS, FF), jnp.float32).at[old_expert].add(slot_grad)
    first_new = BETA_FIRST * first_moment + (1.0 - BETA_FIRST) * gradient
    second_new = BETA_SECOND * second_moment + (1.0 - BETA_SECOND) * gradient * gradient
    weight_old = master_weight.astype(jnp.float32)
    update = first_new / CORRECT_FIRST / (jnp.sqrt(second_new / CORRECT_SECOND) + EPSILON) + DECAY_RATE * weight_old
    weight_new = (weight_old - LEARNING_RATE * update).astype(jnp.bfloat16)
    holder = jnp.full((POSITIONS,), -1, jnp.int32).at[new_place.astype(jnp.int32)].set(new_expert)
    filled = (holder >= 0)[:, None, None]
    source = jnp.maximum(holder, 0)
    slot_weight = jnp.where(filled, weight_new[source], jnp.zeros((), jnp.bfloat16))
    slot_first = jnp.where(filled, first_new[source], jnp.zeros((), jnp.float32))
    slot_second = jnp.where(filled, second_new[source], jnp.zeros((), jnp.float32))
    return (slot_weight, slot_first, slot_second)
```

```python
import functools

import jax
import jax.numpy as jnp
from jax import lax
from jax.experimental import pallas as pl
from jax.experimental.pallas import tpu as pltpu
from jax.sharding import PartitionSpec as P

BETA_FIRST = 0.9
BETA_SECOND = 0.95
LEARNING_RATE = 0.1
DECAY_RATE = 0.1
EPSILON = 1e-08
CORRECT_FIRST = 1.0 - 0.9**10
CORRECT_SECOND = 1.0 - 0.95**10

MESH = pl.DeviceIdType.MESH
LANES = 128
F32 = jnp.float32
BF16 = jnp.bfloat16


def dot(a, b):
    return jnp.dot(a, b, preferred_element_type=F32)


def dot_nt(a, b):
    return lax.dot_general(a, b, (((1,), (1,)), ((), ())), preferred_element_type=F32)


def equal(a, b):
    return jnp.where(a == b, 1.0, 0.0)


def iota(shape, axis):
    return lax.broadcasted_iota(jnp.int32, shape, axis)


def exchange(
    nodes,
    ring,
    meta_ref,
    weight_ref,
    first_ref,
    second_ref,
    features_ref,
    grad_ref,
    out_weight,
    out_first,
    out_second,
    out_grad,
    turned,
    ring_send,
    ring_recv,
    state_send,
    state_recv,
    rows_send,
    rows_recv,
    slots_send,
    slots_recv,
    total,
    order,
    match,
    ring_out_sem,
    ring_in_sem,
    out_sem,
    in_sem,
):
    node = lax.axis_index("node")
    place = lax.axis_index("local")
    experts = weight_ref.shape[0] // 4
    rows = features_ref.shape[2]
    columns = 2 * LANES
    tall = 8 * nodes
    half = ring // 2

    barrier = pltpu.get_barrier_semaphore()

    def greet(k, carry):
        pl.semaphore_signal(
            barrier, inc=1, device_id=(lax.rem(node + k, nodes), place), device_id_type=MESH
        )
        return carry

    lax.fori_loop(1, nodes, greet, 0)
    right = lax.rem(place + 1, ring)
    left = lax.rem(place + ring - 1, ring)
    for neighbour in (right, left):
        pl.semaphore_signal(barrier, inc=1, device_id=(node, neighbour), device_id_type=MESH)

    for c in range(2):
        turned[c] = features_ref[c].astype(F32).T.astype(BF16)

    def partial(c, ahead):
        block = lax.rem(place + ahead + ring, ring)
        at = pl.multiple_of(block * columns, columns)
        return dot(turned[c], grad_ref[c, :, pl.ds(at, columns)])

    chains = {(0, 1): half, (1, -1): half, (0, -1): half - 1, (1, 1): half - 1}
    slot = {}
    for key, length in chains.items():
        for k in range(length):
            slot[key + (k,)] = len(slot)

    def hop(c, way, k):
        j = slot[(c, way, k)]
        return pltpu.make_async_remote_copy(
            src_ref=ring_send.at[j],
            dst_ref=ring_recv.at[j],
            send_sem=ring_out_sem.at[j],
            recv_sem=ring_in_sem.at[j],
            device_id=(node, right if way == 1 else left),
            device_id_type=MESH,
        )

    def advance(c, way, k):
        if k >= chains[(c, way)]:
            return
        value = partial(c, way * (chains[(c, way)] - k))
        if k:
            hop(c, way, k - 1).wait_recv()
            value = value + ring_recv[slot[(c, way, k - 1)]].astype(F32)
        ring_send[slot[(c, way, k)]] = value.astype(BF16)
        if k:
            hop(c, way, k).start()

    for c, way in chains:
        advance(c, way, 0)
    pl.semaphore_wait(barrier, nodes + 1)
    for c, way in chains:
        hop(c, way, 0).start()

    def scatter(send, recv, which, first, last):
        def one(k, carry):
            other = lax.rem(node + k, nodes)
            pltpu.make_async_remote_copy(
                src_ref=send.at[other],
                dst_ref=recv.at[node],
                send_sem=out_sem.at[which],
                recv_sem=in_sem.at[which],
                device_id=(other, place),
                device_id_type=MESH,
            ).start()
            return carry

        lax.fori_loop(first, last, one, 0)

    def all_but_one(send, recv, which):
        return pltpu.make_async_remote_copy(
            src_ref=send.at[pl.ds(0, nodes - 1)],
            dst_ref=recv.at[pl.ds(0, nodes - 1)],
            send_sem=out_sem.at[which],
            recv_sem=in_sem.at[which],
            device_id=(lax.rem(node + 1, nodes), place),
            device_id_type=MESH,
        )

    old_place, old_expert = meta_ref[0:1, :], meta_ref[1:2, :]
    new_place, new_expert = meta_ref[2:3, :], meta_ref[3:4, :]
    slots = meta_ref.shape[1]
    position = iota((tall, slots), 0) // 4
    at_new = equal(position, new_place).astype(BF16)
    own_row = equal(iota((4 * experts, slots), 0) // 4, new_expert).astype(BF16)
    choose = dot_nt(at_new, own_row)
    same = (iota((tall, 4 * experts), 0) % 4) == (iota((tall, 4 * experts), 1) % 4)
    choose = jnp.where(same, choose, 0.0).astype(BF16)
    for a, ref in enumerate((weight_ref, first_ref, second_ref)):
        picked = dot(choose, ref[...].astype(BF16))
        state_send[:, a] = picked.reshape(nodes, 8, LANES).astype(BF16)
    quarter = nodes // 4
    scatter(state_send, state_recv, 0, 1, quarter)
    for c, way in chains:
        advance(c, way, 1)
    scatter(state_send, state_recv, 0, quarter, 2 * quarter)
    state_recv[node] = state_send[node]
    for c, way in chains:
        advance(c, way, 2)
    scatter(state_send, state_recv, 0, 2 * quarter, 3 * quarter)

    at_old = equal(position, old_place).astype(BF16)
    expert = iota((experts, slots), 0)
    held_new = dot_nt(at_new, equal(expert, new_expert).astype(BF16)).astype(BF16)
    held_old = dot_nt(at_old, equal(expert, old_expert).astype(BF16)).astype(BF16)
    pairs = dot_nt(held_new, held_old)
    tall_row, tall_column = iota((tall, tall), 0), iota((tall, tall), 1)
    match[...] = jnp.where((tall_row % 4) == (tall_column % 4), pairs, 0.0).astype(BF16)
    q, r = tall_row // rows, tall_row % rows
    order[...] = equal(tall_column, (r // 2) * 8 + q * 2 + r % 2).astype(BF16)
    for k in range(3, half):
        for c, way in chains:
            advance(c, way, k)
    scatter(state_send, state_recv, 0, 3 * quarter, nodes)

    for c in range(2):
        value = partial(c, 0)
        for way in (1, -1):
            k = chains[(c, way)] - 1
            hop(c, way, k).wait_recv()
            value = value + ring_recv[slot[(c, way, k)]].astype(F32)
        for h in range(2):
            total[pl.ds((2 * c + h) * rows, rows), :] = value[:, h * LANES : (h + 1) * LANES].astype(BF16)
    mine = lax.dot_general(
        order[...], total[...], (((0,), (0,)), ((), ())), preferred_element_type=F32
    )
    rows_send[...] = mine.reshape(nodes, 8, LANES).astype(BF16)
    scatter(rows_send, rows_recv, 1, 1, nodes)
    rows_recv[node] = rows_send[node]

    def natural(block, out):
        value = dot(order[...], block.astype(F32).reshape(tall, LANES).astype(BF16))
        for c in range(2):
            for h in range(2):
                out[c, :, h * LANES : (h + 1) * LANES] = value[
                    (2 * c + h) * rows : (2 * c + h + 1) * rows
                ].astype(BF16)

    all_but_one(state_send, state_recv, 0).wait_recv()
    for a, out in enumerate((out_weight, out_first, out_second)):
        natural(state_recv[:, a], out)

    all_but_one(rows_send, rows_recv, 1).wait_recv()
    summed = dot(match[...], rows_recv[...].astype(F32).reshape(tall, LANES).astype(BF16))
    slots_send[...] = summed.reshape(nodes, 8, LANES).astype(BF16)
    scatter(slots_send, slots_recv, 2, 1, nodes)
    slots_recv[node] = slots_send[node]

    for key, length in chains.items():
        for k in range(length):
            hop(*key, k).wait_send()
    all_but_one(state_send, state_recv, 0).wait_send()
    all_but_one(rows_send, rows_recv, 1).wait_send()
    all_but_one(slots_send, slots_recv, 2).wait_recv()
    natural(slots_recv[...], out_grad)
    all_but_one(slots_send, slots_recv, 2).wait_send()


def by_row(state):
    experts = state.shape[0]
    return state.reshape(experts, 2, 2, LANES).transpose(0, 2, 1, 3).reshape(4 * experts, LANES)


def local(
    master_weight,
    first_moment,
    second_moment,
    features,
    grad_out,
    old_place,
    new_place,
    old_owner,
    new_owner,
):
    nodes, ring = lax.axis_size("node"), lax.axis_size("local")
    experts = master_weight.shape[0]
    rows = features.shape[3]
    columns = master_weight.shape[2]
    primaries = jnp.arange(experts, dtype=jnp.int32)
    meta = jnp.stack(
        [
            old_place,
            jnp.concatenate([primaries, old_owner]),
            new_place,
            jnp.concatenate([primaries, new_owner]),
        ]
    )
    tall = 8 * nodes
    hops = 2 * (ring - 1)
    vmem = pl.BlockSpec(memory_space=pltpu.VMEM)
    block = jax.ShapeDtypeStruct((2, rows, columns), BF16)
    weight_old, first_old, second_old, gradient = pl.pallas_call(
        functools.partial(exchange, nodes, ring),
        out_shape=(block,) * 4,
        in_specs=[vmem] * 6,
        out_specs=(vmem,) * 4,
        scratch_shapes=[
            pltpu.VMEM((2, rows, features.shape[2]), BF16),
            pltpu.VMEM((hops, rows, columns), BF16),
            pltpu.VMEM((hops, rows, columns), BF16),
            pltpu.VMEM((nodes, 3, 8, LANES), BF16),
            pltpu.VMEM((nodes, 3, 8, LANES), BF16),
            pltpu.VMEM((nodes, 8, LANES), BF16),
            pltpu.VMEM((nodes, 8, LANES), BF16),
            pltpu.VMEM((nodes, 8, LANES), BF16),
            pltpu.VMEM((nodes, 8, LANES), BF16),
            pltpu.VMEM((tall, LANES), BF16),
            pltpu.VMEM((tall, tall), BF16),
            pltpu.VMEM((tall, tall), BF16),
            pltpu.SemaphoreType.DMA((hops,)),
            pltpu.SemaphoreType.DMA((hops,)),
            pltpu.SemaphoreType.DMA((3,)),
            pltpu.SemaphoreType.DMA((3,)),
        ],
        compiler_params=pltpu.CompilerParams(
            collective_id=0, has_side_effects=True, vmem_limit_bytes=32 * 1024 * 1024
        ),
        name="exchange",
    )(
        meta,
        by_row(master_weight),
        by_row(first_moment),
        by_row(second_moment),
        features.reshape(2, features.shape[2], rows),
        grad_out.reshape(2, grad_out.shape[2], grad_out.shape[3]),
    )
    gradient = gradient.astype(F32)
    first_new = BETA_FIRST * first_old.astype(F32) + (1.0 - BETA_FIRST) * gradient
    second_new = BETA_SECOND * second_old.astype(F32) + (1.0 - BETA_SECOND) * gradient * gradient
    weight_old = weight_old.astype(F32)
    update = (
        first_new / CORRECT_FIRST / (jnp.sqrt(second_new / CORRECT_SECOND) + EPSILON)
        + DECAY_RATE * weight_old
    )
    weight_new = (weight_old - LEARNING_RATE * update).astype(BF16)
    return weight_new, first_new, second_new


def solution(mesh):
    return jax.shard_map(
        local,
        mesh=mesh,
        in_specs=(
            P(None, "node", "local"),
            P(None, "node", "local"),
            P(None, "node", "local"),
            P("node", "local", None, None),
            P("node", "local", None, None),
            P(),
            P(),
            P(),
            P(),
        ),
        out_specs=(P("node", None, "local"), P("node", None, "local"), P("node", None, "local")),
        check_vma=False,
    )
```

```python
import functools

import jax
import jax.numpy as jnp
from jax import lax
from jax.experimental import pallas as pl
from jax.experimental.pallas import tpu as pltpu
from jax.sharding import PartitionSpec as P

BETA_FIRST = 0.9
BETA_SECOND = 0.95
LEARNING_RATE = 0.1
DECAY_RATE = 0.1
EPSILON = 1e-08
CORRECT_FIRST = 1.0 - 0.9**10
CORRECT_SECOND = 1.0 - 0.95**10

MESH = pl.DeviceIdType.MESH
LANES = 128
CHUNKS = 4
F32 = jnp.float32
BF16 = jnp.bfloat16


def dot(a, b):
    return jnp.dot(a, b, preferred_element_type=F32)


def dot_nt(a, b):
    return lax.dot_general(a, b, (((1,), (1,)), ((), ())), preferred_element_type=F32)


def equal(a, b):
    return jnp.where(a == b, 1.0, 0.0)


def iota(shape, axis):
    return lax.broadcasted_iota(jnp.int32, shape, axis)


def exchange(
    nodes,
    ring,
    old_place_hbm,
    new_place_hbm,
    old_owner_hbm,
    new_owner_hbm,
    weight_hbm,
    first_hbm,
    second_hbm,
    features_hbm,
    grad_hbm,
    out_weight,
    out_first,
    out_second,
    out_grad,
    old_place_ref,
    new_place_ref,
    old_owner_ref,
    new_owner_ref,
    weight_ref,
    first_ref,
    second_ref,
    features_ref,
    grad_ref,
    load_sem,
    turned,
    ring_send,
    ring_recv,
    state_send,
    state_recv,
    rows_send,
    rows_recv,
    slots_send,
    slots_recv,
    parts,
    total,
    piece_order,
    order,
    match,
    ring_out_sem,
    ring_in_sem,
    out_sem,
    in_sem,
):
    node = lax.axis_index("node")
    place = lax.axis_index("local")
    experts = weight_ref.shape[0] // 4
    rows = features_ref.shape[2]
    columns = 2 * LANES
    tall = 8 * nodes
    half = ring // 2
    loads = [
        pltpu.make_async_copy(source, target, load_sem.at[i])
        for i, (source, target) in enumerate(
            (
                (features_hbm, features_ref),
                (grad_hbm, grad_ref),
                (new_place_hbm, new_place_ref),
                (new_owner_hbm, new_owner_ref),
                (weight_hbm, weight_ref),
                (first_hbm, first_ref),
                (second_hbm, second_ref),
                (old_place_hbm, old_place_ref),
                (old_owner_hbm, old_owner_ref),
            )
        )
    ]

    barrier = pltpu.get_barrier_semaphore()

    def greet(k, carry):
        pl.semaphore_signal(
            barrier, inc=1, device_id=(lax.rem(node + k, nodes), place), device_id_type=MESH
        )
        return carry

    lax.fori_loop(1, nodes, greet, 0)
    right = lax.rem(place + 1, ring)
    left = lax.rem(place + ring - 1, ring)
    for neighbour in (right, left):
        pl.semaphore_signal(barrier, inc=1, device_id=(node, neighbour), device_id_type=MESH)

    for load in loads:
        load.start()
    for load in loads[:2]:
        load.wait()
    for c in range(2):
        turned[c] = features_ref[c].astype(F32).T.astype(BF16)

    def partial(c, ahead):
        block = lax.rem(place + ahead + ring, ring)
        at = pl.multiple_of(block * columns, columns)
        return dot(turned[c], grad_ref[c, :, pl.ds(at, columns)])

    chains = {(0, 1): half, (1, -1): half, (0, -1): half - 1, (1, 1): half - 1}
    slot = {}
    for key, length in chains.items():
        for k in range(length):
            slot[key + (k,)] = len(slot)
    piece = rows // CHUNKS

    def hop(c, way, k, j):
        at = slot[(c, way, k)]
        return pltpu.make_async_remote_copy(
            src_ref=ring_send.at[j, at],
            dst_ref=ring_recv.at[j, at],
            send_sem=ring_out_sem.at[j, at],
            recv_sem=ring_in_sem.at[j, at],
            device_id=(node, right if way == 1 else left),
            device_id_type=MESH,
        )

    def advance(c, way, k, j):
        at = slot[(c, way, k)]
        hop(c, way, k - 1, j).wait_recv()
        value = parts[at, pl.ds(j * piece, piece), :] + ring_recv[j, slot[(c, way, k - 1)]].astype(F32)
        ring_send[j, at] = value.astype(BF16)
        hop(c, way, k, j).start()

    for c, way in chains:
        value = partial(c, way * chains[(c, way)]).astype(BF16)
        for j in range(CHUNKS):
            ring_send[j, slot[(c, way, 0)]] = value[j * piece : (j + 1) * piece]
    pl.semaphore_wait(barrier, nodes + 1)
    for j in range(CHUNKS):
        for c, way in chains:
            hop(c, way, 0, j).start()
    for (c, way, k), at in slot.items():
        if k:
            parts[at] = partial(c, way * (chains[(c, way)] - k))
    for c in range(2):
        parts[slot[(c, 1, 0)]] = partial(c, 0)

    def scatter(send, recv, which, first, last):
        def one(k, carry):
            other = lax.rem(node + k, nodes)
            pltpu.make_async_remote_copy(
                src_ref=send.at[other],
                dst_ref=recv.at[node],
                send_sem=out_sem.at[which],
                recv_sem=in_sem.at[which],
                device_id=(other, place),
                device_id_type=MESH,
            ).start()
            return carry

        lax.fori_loop(first, last, one, 0)

    def all_but_one(send, recv, which):
        return pltpu.make_async_remote_copy(
            src_ref=send.at[pl.ds(0, nodes - 1)],
            dst_ref=recv.at[pl.ds(0, nodes - 1)],
            send_sem=out_sem.at[which],
            recv_sem=in_sem.at[which],
            device_id=(lax.rem(node + 1, nodes), place),
            device_id_type=MESH,
        )

    for load in loads[2:]:
        load.wait()
    redundant = old_owner_ref.shape[1]
    slots = experts + redundant
    position = iota((tall, slots), 0) // 4

    def expert_of_slot(owner, repeat):
        owned = equal(iota((experts * repeat, redundant), 0) // repeat, owner).astype(BF16)
        tail = equal(iota((redundant, slots), 0) + experts, iota((redundant, slots), 1)).astype(BF16)
        primary = equal(iota((experts * repeat, slots), 0) // repeat, iota((experts * repeat, slots), 1))
        return (dot(owned, tail) + primary).astype(BF16)

    at_new = equal(position, new_place_ref[...]).astype(BF16)
    choose = dot_nt(at_new, expert_of_slot(new_owner_ref[...], 4))
    same = (iota((tall, 4 * experts), 0) % 4) == (iota((tall, 4 * experts), 1) % 4)
    choose = jnp.where(same, choose, 0.0).astype(BF16)
    for a, ref in enumerate((weight_ref, first_ref, second_ref)):
        picked = dot(choose, ref[...].astype(BF16))
        state_send[:, a] = picked.reshape(nodes, 8, LANES).astype(BF16)
    state_recv[node] = state_send[node]
    steps = (half - 1) * CHUNKS
    bounds = [1 + (nodes - 1) * i // steps for i in range(steps + 1)]
    for k in range(1, half):
        for j in range(CHUNKS):
            for c, way in chains:
                if k < chains[(c, way)]:
                    advance(c, way, k, j)
            i = (k - 1) * CHUNKS + j
            scatter(state_send, state_recv, 0, bounds[i], bounds[i + 1])
        if k == 1:
            at_old = equal(position, old_place_ref[...]).astype(BF16)
            held_new = dot_nt(at_new, expert_of_slot(new_owner_ref[...], 1)).astype(BF16)
            held_old = dot_nt(at_old, expert_of_slot(old_owner_ref[...], 1)).astype(BF16)
            pairs = dot_nt(held_new, held_old)
            tall_row, tall_column = iota((tall, tall), 0), iota((tall, tall), 1)
            match[...] = jnp.where((tall_row % 4) == (tall_column % 4), pairs, 0.0).astype(BF16)
        if k == 2:
            q, r = tall_row // rows, tall_row % rows
            order[0] = equal(tall_column, (r // 2) * 8 + q * 2 + r % 2).astype(BF16)
            owner = (r % piece) // 2 * CHUNKS + r // piece
            order[1] = equal(tall_column, owner * 8 + q * 2 + r % 2).astype(BF16)
            short = 4 * piece
            short_row, short_column = iota((short, short), 0), iota((short, short), 1)
            q, r = short_column // piece, short_column % piece
            piece_order[...] = equal(short_row, (r // 2) * 8 + q * 2 + r % 2).astype(BF16)

    group = nodes // CHUNKS
    for j in range(CHUNKS):
        for c in range(2):
            value = parts[slot[(c, 1, 0)], pl.ds(j * piece, piece), :]
            for way in (1, -1):
                k = chains[(c, way)] - 1
                hop(c, way, k, j).wait_recv()
                value = value + ring_recv[j, slot[(c, way, k)]].astype(F32)
            value = value.astype(BF16)
            for h in range(2):
                total[j, pl.ds((2 * c + h) * piece, piece), :] = value[:, h * LANES : (h + 1) * LANES]
        mine = dot(piece_order[...], total[j])
        rows_send[j] = mine.reshape(group, 8, LANES).astype(BF16)

        def give(k, carry, j=j):
            at = lax.rem(node // CHUNKS + k, group)
            pltpu.make_async_remote_copy(
                src_ref=rows_send.at[j, at],
                dst_ref=rows_recv.at[node],
                send_sem=out_sem.at[1],
                recv_sem=in_sem.at[1],
                device_id=(at * CHUNKS + j, place),
                device_id_type=MESH,
            ).start()
            return carry

        lax.fori_loop(1, group, give, 0)

        @pl.when(lax.rem(node, CHUNKS) != j)
        def _(give=give):
            give(0, 0)

    rows_recv[node] = rows_send[lax.rem(node, CHUNKS), node // CHUNKS]

    def natural(block, out, which):
        value = dot(order[which], block.astype(F32).reshape(tall, LANES).astype(BF16))
        for c in range(2):
            for h in range(2):
                out[c, :, h * LANES : (h + 1) * LANES] = value[
                    (2 * c + h) * rows : (2 * c + h + 1) * rows
                ].astype(BF16)

    all_but_one(state_send, state_recv, 0).wait_recv()
    for a, out in enumerate((out_weight, out_first, out_second)):
        natural(state_recv[:, a], out, 0)

    all_but_one(rows_recv, rows_recv, 1).wait_recv()
    summed = dot(match[...], rows_recv[...].astype(F32).reshape(tall, LANES).astype(BF16))
    slots_send[...] = summed.reshape(nodes, 8, LANES).astype(BF16)
    scatter(slots_send, slots_recv, 2, 1, nodes)
    slots_recv[node] = slots_send[node]

    for key, length in chains.items():
        for k in range(length):
            for j in range(CHUNKS):
                hop(*key, k, j).wait_send()
    all_but_one(state_send, state_recv, 0).wait_send()
    all_but_one(rows_recv, rows_recv, 1).wait_send()
    all_but_one(slots_send, slots_recv, 2).wait_recv()
    natural(slots_recv[...], out_grad, 1)
    all_but_one(slots_send, slots_recv, 2).wait_send()


def by_row(state):
    experts = state.shape[0]
    return state.reshape(experts, 2, 2, LANES).transpose(0, 2, 1, 3).reshape(4 * experts, LANES)


def local(
    master_weight,
    first_moment,
    second_moment,
    features,
    grad_out,
    old_place,
    new_place,
    old_owner,
    new_owner,
):
    nodes, ring = lax.axis_size("node"), lax.axis_size("local")
    experts = master_weight.shape[0]
    rows = features.shape[3]
    columns = master_weight.shape[2]
    tall = 8 * nodes
    hops = 2 * (ring - 1)
    piece = rows // CHUNKS
    operands = (
        old_place.reshape(1, -1),
        new_place.reshape(1, -1),
        old_owner.reshape(1, -1),
        new_owner.reshape(1, -1),
        by_row(master_weight),
        by_row(first_moment),
        by_row(second_moment),
        features.reshape(2, features.shape[2], rows),
        grad_out.reshape(2, grad_out.shape[2], grad_out.shape[3]),
    )
    vmem = pl.BlockSpec(memory_space=pltpu.VMEM)
    block = jax.ShapeDtypeStruct((2, rows, columns), BF16)
    weight_old, first_old, second_old, gradient = pl.pallas_call(
        functools.partial(exchange, nodes, ring),
        out_shape=(block,) * 4,
        in_specs=[pl.BlockSpec(memory_space=pltpu.HBM)] * len(operands),
        out_specs=(vmem,) * 4,
        scratch_shapes=[
            *(pltpu.VMEM(operand.shape, operand.dtype) for operand in operands),
            pltpu.SemaphoreType.DMA((len(operands),)),
            pltpu.VMEM((2, rows, features.shape[2]), BF16),
            pltpu.VMEM((CHUNKS, hops, piece, columns), BF16),
            pltpu.VMEM((CHUNKS, hops, piece, columns), BF16),
            pltpu.VMEM((nodes, 3, 8, LANES), BF16),
            pltpu.VMEM((nodes, 3, 8, LANES), BF16),
            pltpu.VMEM((CHUNKS, nodes // CHUNKS, 8, LANES), BF16),
            pltpu.VMEM((nodes, 8, LANES), BF16),
            pltpu.VMEM((nodes, 8, LANES), BF16),
            pltpu.VMEM((nodes, 8, LANES), BF16),
            pltpu.VMEM((hops, rows, columns), F32),
            pltpu.VMEM((CHUNKS, 4 * piece, LANES), BF16),
            pltpu.VMEM((4 * piece, 4 * piece), BF16),
            pltpu.VMEM((2, tall, tall), BF16),
            pltpu.VMEM((tall, tall), BF16),
            pltpu.SemaphoreType.DMA((CHUNKS, hops)),
            pltpu.SemaphoreType.DMA((CHUNKS, hops)),
            pltpu.SemaphoreType.DMA((3,)),
            pltpu.SemaphoreType.DMA((3,)),
        ],
        compiler_params=pltpu.CompilerParams(
            collective_id=0, has_side_effects=True, vmem_limit_bytes=60 * 1024 * 1024
        ),
        name="exchange",
    )(*operands)
    gradient = gradient.astype(F32)
    first_new = BETA_FIRST * first_old.astype(F32) + (1.0 - BETA_FIRST) * gradient
    second_new = BETA_SECOND * second_old.astype(F32) + (1.0 - BETA_SECOND) * gradient * gradient
    weight_old = weight_old.astype(F32)
    update = (
        first_new / CORRECT_FIRST / (jnp.sqrt(second_new / CORRECT_SECOND) + EPSILON)
        + DECAY_RATE * weight_old
    )
    weight_new = (weight_old - LEARNING_RATE * update).astype(BF16)
    return weight_new, first_new, second_new


def solution(mesh):
    return jax.shard_map(
        local,
        mesh=mesh,
        in_specs=(
            P(None, "node", "local"),
            P(None, "node", "local"),
            P(None, "node", "local"),
            P("node", "local", None, None),
            P("node", "local", None, None),
            P(),
            P(),
            P(),
            P(),
        ),
        out_specs=(P("node", None, "local"), P("node", None, "local"), P("node", None, "local")),
        check_vma=False,
    )
```

```python
import functools

import jax
import jax.numpy as jnp
from jax import lax
from jax.experimental import pallas as pl
from jax.experimental.pallas import tpu as pltpu
from jax.sharding import PartitionSpec as P

BETA_FIRST = 0.9
BETA_SECOND = 0.95
LEARNING_RATE = 0.1
DECAY_RATE = 0.1
EPSILON = 1e-08
CORRECT_FIRST = 1.0 - 0.9**10
CORRECT_SECOND = 1.0 - 0.95**10

MESH = pl.DeviceIdType.MESH
LANES = 128
CHUNKS = 4
CHIPS_X, CHIPS_Z = 4, 8
F32 = jnp.float32
BF16 = jnp.bfloat16


def dot(a, b):
    return jnp.dot(a, b, preferred_element_type=F32)


def dot_nt(a, b):
    return lax.dot_general(a, b, (((1,), (1,)), ((), ())), preferred_element_type=F32)


def equal(a, b):
    return jnp.where(a == b, 1.0, 0.0)


def iota(shape, axis):
    return lax.broadcasted_iota(jnp.int32, shape, axis)


def exchange(
    nodes,
    ring,
    old_place_hbm,
    new_place_hbm,
    old_owner_hbm,
    new_owner_hbm,
    weight_hbm,
    first_hbm,
    second_hbm,
    features_hbm,
    grad_hbm,
    out_weight,
    out_first,
    out_second,
    out_grad,
    old_place_ref,
    new_place_ref,
    old_owner_ref,
    new_owner_ref,
    weight_ref,
    first_ref,
    second_ref,
    features_ref,
    grad_ref,
    load_sem,
    turned,
    ring_send,
    ring_recv,
    state_send,
    state_recv,
    rows_send,
    rows_recv,
    slots_send,
    slots_recv,
    parts,
    total,
    piece_order,
    order,
    match,
    ring_out_sem,
    ring_in_sem,
    out_sem,
    in_sem,
    round_sem,
):
    node = lax.axis_index("node")
    place = lax.axis_index("local")
    experts = weight_ref.shape[0] // 4
    rows = features_ref.shape[2]
    columns = 2 * LANES
    tall = 8 * nodes
    half = ring // 2
    loads = [
        pltpu.make_async_copy(source, target, load_sem.at[i])
        for i, (source, target) in enumerate(
            (
                (features_hbm, features_ref),
                (grad_hbm, grad_ref),
                (new_place_hbm, new_place_ref),
                (new_owner_hbm, new_owner_ref),
                (weight_hbm, weight_ref),
                (first_hbm, first_ref),
                (second_hbm, second_ref),
                (old_place_hbm, old_place_ref),
                (old_owner_hbm, old_owner_ref),
            )
        )
    ]

    x, z, core = node // (2 * CHIPS_Z), lax.rem(node // 2, CHIPS_Z), lax.rem(node, 2)

    def away(dx, dz, dc):
        to_x = lax.rem(x + dx, CHIPS_X) if dx else x
        to_z = lax.rem(z + dz, CHIPS_Z) if dz else z
        return (to_x * CHIPS_Z + to_z) * 2 + (1 - core if dc else core)

    def distance(offset):
        dx, dz = offset[0], offset[1]
        return min(dx, CHIPS_X - dx) + min(dz, CHIPS_Z - dz)

    offsets = [(dx, dz, dc) for dx in range(CHIPS_X) for dz in range(CHIPS_Z) for dc in range(2)][1:]
    offsets.sort(key=distance, reverse=True)
    farthest = distance(offsets[0])
    next_to = [(1, 0), (CHIPS_X - 1, 0), (0, 1), (0, CHIPS_Z - 1)]

    barrier = pltpu.get_barrier_semaphore()
    right = lax.rem(place + 1, ring)
    left = lax.rem(place + ring - 1, ring)
    for neighbour in (right, left):
        pl.semaphore_signal(barrier, inc=1, device_id=(node, neighbour), device_id_type=MESH)
    close = [(0, 0, 1)] + [(dx, dz, dc) for dx, dz in next_to for dc in range(2)]
    for offset in close:
        pl.semaphore_signal(barrier, inc=1, device_id=(away(*offset), place), device_id_type=MESH)

    def tell(r):
        for dx, dz in next_to:
            pl.semaphore_signal(
                round_sem.at[r - 1], inc=1, device_id=(away(dx, dz, 0), place), device_id_type=MESH
            )

    def hear(r):
        pl.semaphore_wait(round_sem.at[r - 1], len(next_to))

    for load in loads:
        load.start()
    for load in loads[:2]:
        load.wait()
    for c in range(2):
        turned[c] = features_ref[c].astype(F32).T.astype(BF16)

    def partial(c, ahead):
        block = lax.rem(place + ahead + ring, ring)
        at = pl.multiple_of(block * columns, columns)
        return dot(turned[c], grad_ref[c, :, pl.ds(at, columns)])

    chains = {(0, 1): half, (1, -1): half, (0, -1): half - 1, (1, 1): half - 1}
    slot = {}
    for key, length in chains.items():
        for k in range(length):
            slot[key + (k,)] = len(slot)
    piece = rows // CHUNKS

    def hop(c, way, k, j):
        at = slot[(c, way, k)]
        return pltpu.make_async_remote_copy(
            src_ref=ring_send.at[j, at],
            dst_ref=ring_recv.at[j, at],
            send_sem=ring_out_sem.at[j, at],
            recv_sem=ring_in_sem.at[j, at],
            device_id=(node, right if way == 1 else left),
            device_id_type=MESH,
        )

    def advance(c, way, k, j):
        at = slot[(c, way, k)]
        hop(c, way, k - 1, j).wait_recv()
        value = parts[at, pl.ds(j * piece, piece), :] + ring_recv[j, slot[(c, way, k - 1)]].astype(F32)
        ring_send[j, at] = value.astype(BF16)
        hop(c, way, k, j).start()

    for c, way in chains:
        value = partial(c, way * chains[(c, way)]).astype(BF16)
        for j in range(CHUNKS):
            ring_send[j, slot[(c, way, 0)]] = value[j * piece : (j + 1) * piece]
    pl.semaphore_wait(barrier, 2 + len(close))
    for j in range(CHUNKS):
        for c, way in chains:
            hop(c, way, 0, j).start()
    tell(1)
    for (c, way, k), at in slot.items():
        if k:
            parts[at] = partial(c, way * (chains[(c, way)] - k))
    for c in range(2):
        parts[slot[(c, 1, 0)]] = partial(c, 0)

    def scatter(send, recv, which, some):
        for offset in some:
            other = away(*offset)
            pltpu.make_async_remote_copy(
                src_ref=send.at[other],
                dst_ref=recv.at[node],
                send_sem=out_sem.at[which],
                recv_sem=in_sem.at[which],
                device_id=(other, place),
                device_id_type=MESH,
            ).start()

    def state_up_to(low, high):
        scatter(state_send, state_recv, 0, [o for o in offsets if low <= distance(o) <= high])

    def all_but_one(send, recv, which):
        return pltpu.make_async_remote_copy(
            src_ref=send.at[pl.ds(0, nodes - 1)],
            dst_ref=recv.at[pl.ds(0, nodes - 1)],
            send_sem=out_sem.at[which],
            recv_sem=in_sem.at[which],
            device_id=(lax.rem(node + 1, nodes), place),
            device_id_type=MESH,
        )

    for load in loads[2:]:
        load.wait()
    redundant = old_owner_ref.shape[1]
    slots = experts + redundant
    position = iota((tall, slots), 0) // 4

    def expert_of_slot(owner, repeat):
        owned = equal(iota((experts * repeat, redundant), 0) // repeat, owner).astype(BF16)
        tail = equal(iota((redundant, slots), 0) + experts, iota((redundant, slots), 1)).astype(BF16)
        primary = equal(iota((experts * repeat, slots), 0) // repeat, iota((experts * repeat, slots), 1))
        return (dot(owned, tail) + primary).astype(BF16)

    at_new = equal(position, new_place_ref[...]).astype(BF16)
    choose = dot_nt(at_new, expert_of_slot(new_owner_ref[...], 4))
    same = (iota((tall, 4 * experts), 0) % 4) == (iota((tall, 4 * experts), 1) % 4)
    choose = jnp.where(same, choose, 0.0).astype(BF16)
    for a, ref in enumerate((weight_ref, first_ref, second_ref)):
        picked = dot(choose, ref[...].astype(BF16))
        state_send[:, a] = picked.reshape(nodes, 8, LANES).astype(BF16)
    state_recv[node] = state_send[node]
    state_up_to(0, 1)
    last_step = (half - 1) * CHUNKS - 1
    heard = 0
    for k in range(1, half):
        for j in range(CHUNKS):
            for c, way in chains:
                if k < chains[(c, way)]:
                    advance(c, way, k, j)
            due = ((k - 1) * CHUNKS + j + 1) * (farthest - 1) // (last_step + 1)
            while heard < due:
                heard += 1
                hear(heard)
                if heard < farthest - 1:
                    tell(heard + 1)
                state_up_to(heard + 1, heard + 1)
        if k == 1:
            at_old = equal(position, old_place_ref[...]).astype(BF16)
            held_new = dot_nt(at_new, expert_of_slot(new_owner_ref[...], 1)).astype(BF16)
            held_old = dot_nt(at_old, expert_of_slot(old_owner_ref[...], 1)).astype(BF16)
            pairs = dot_nt(held_new, held_old)
            tall_row, tall_column = iota((tall, tall), 0), iota((tall, tall), 1)
            match[...] = jnp.where((tall_row % 4) == (tall_column % 4), pairs, 0.0).astype(BF16)
        if k == 2:
            q, r = tall_row // rows, tall_row % rows
            order[0] = equal(tall_column, (r // 2) * 8 + q * 2 + r % 2).astype(BF16)
            owner = (r % piece) // 2 * CHUNKS + r // piece
            order[1] = equal(tall_column, owner * 8 + q * 2 + r % 2).astype(BF16)
            short = 4 * piece
            short_row, short_column = iota((short, short), 0), iota((short, short), 1)
            q, r = short_column // piece, short_column % piece
            piece_order[...] = equal(short_row, (r // 2) * 8 + q * 2 + r % 2).astype(BF16)

    group = nodes // CHUNKS
    line = group // CHIPS_X
    steps = sorted(
        range(group),
        key=lambda k: -distance((k // line, k % line * CHIPS_Z // line)),
    )
    hosts = [
        (
            k,
            lax.rem(node // (line * CHUNKS) + k // line, CHIPS_X) * line
            + lax.rem(node // CHUNKS + k % line, line),
        )
        for k in steps
    ]
    for j in range(CHUNKS):
        for c in range(2):
            value = parts[slot[(c, 1, 0)], pl.ds(j * piece, piece), :]
            for way in (1, -1):
                k = chains[(c, way)] - 1
                hop(c, way, k, j).wait_recv()
                value = value + ring_recv[j, slot[(c, way, k)]].astype(F32)
            value = value.astype(BF16)
            for h in range(2):
                total[j, pl.ds((2 * c + h) * piece, piece), :] = value[:, h * LANES : (h + 1) * LANES]
        mine = dot(piece_order[...], total[j])
        rows_send[j] = mine.reshape(group, 8, LANES).astype(BF16)

        for step, at in hosts:
            copy = pltpu.make_async_remote_copy(
                src_ref=rows_send.at[j, at],
                dst_ref=rows_recv.at[node],
                send_sem=out_sem.at[1],
                recv_sem=in_sem.at[1],
                device_id=(at * CHUNKS + j, place),
                device_id_type=MESH,
            )
            if step:
                copy.start()
            else:
                pl.when(lax.rem(node, CHUNKS) != j)(copy.start)

    rows_recv[node] = rows_send[lax.rem(node, CHUNKS), node // CHUNKS]

    def natural(block, out, which):
        value = dot(order[which], block.astype(F32).reshape(tall, LANES).astype(BF16))
        for c in range(2):
            for h in range(2):
                out[c, :, h * LANES : (h + 1) * LANES] = value[
                    (2 * c + h) * rows : (2 * c + h + 1) * rows
                ].astype(BF16)

    all_but_one(state_send, state_recv, 0).wait_recv()
    for a, out in enumerate((out_weight, out_first, out_second)):
        natural(state_recv[:, a], out, 0)

    all_but_one(rows_recv, rows_recv, 1).wait_recv()
    summed = dot(match[...], rows_recv[...].astype(F32).reshape(tall, LANES).astype(BF16))
    slots_send[...] = summed.reshape(nodes, 8, LANES).astype(BF16)
    scatter(slots_send, slots_recv, 2, offsets)
    slots_recv[node] = slots_send[node]

    for key, length in chains.items():
        for k in range(length):
            for j in range(CHUNKS):
                hop(*key, k, j).wait_send()
    all_but_one(state_send, state_recv, 0).wait_send()
    all_but_one(rows_recv, rows_recv, 1).wait_send()
    all_but_one(slots_send, slots_recv, 2).wait_recv()
    natural(slots_recv[...], out_grad, 1)
    all_but_one(slots_send, slots_recv, 2).wait_send()


def by_row(state):
    experts = state.shape[0]
    return state.reshape(experts, 2, 2, LANES).transpose(0, 2, 1, 3).reshape(4 * experts, LANES)


def local(
    master_weight,
    first_moment,
    second_moment,
    features,
    grad_out,
    old_place,
    new_place,
    old_owner,
    new_owner,
):
    nodes, ring = lax.axis_size("node"), lax.axis_size("local")
    experts = master_weight.shape[0]
    rows = features.shape[3]
    columns = master_weight.shape[2]
    tall = 8 * nodes
    hops = 2 * (ring - 1)
    piece = rows // CHUNKS
    operands = (
        old_place.reshape(1, -1),
        new_place.reshape(1, -1),
        old_owner.reshape(1, -1),
        new_owner.reshape(1, -1),
        by_row(master_weight),
        by_row(first_moment),
        by_row(second_moment),
        features.reshape(2, features.shape[2], rows),
        grad_out.reshape(2, grad_out.shape[2], grad_out.shape[3]),
    )
    vmem = pl.BlockSpec(memory_space=pltpu.VMEM)
    block = jax.ShapeDtypeStruct((2, rows, columns), BF16)
    weight_old, first_old, second_old, gradient = pl.pallas_call(
        functools.partial(exchange, nodes, ring),
        out_shape=(block,) * 4,
        in_specs=[pl.BlockSpec(memory_space=pltpu.HBM)] * len(operands),
        out_specs=(vmem,) * 4,
        scratch_shapes=[
            *(pltpu.VMEM(operand.shape, operand.dtype) for operand in operands),
            pltpu.SemaphoreType.DMA((len(operands),)),
            pltpu.VMEM((2, rows, features.shape[2]), BF16),
            pltpu.VMEM((CHUNKS, hops, piece, columns), BF16),
            pltpu.VMEM((CHUNKS, hops, piece, columns), BF16),
            pltpu.VMEM((nodes, 3, 8, LANES), BF16),
            pltpu.VMEM((nodes, 3, 8, LANES), BF16),
            pltpu.VMEM((CHUNKS, nodes // CHUNKS, 8, LANES), BF16),
            pltpu.VMEM((nodes, 8, LANES), BF16),
            pltpu.VMEM((nodes, 8, LANES), BF16),
            pltpu.VMEM((nodes, 8, LANES), BF16),
            pltpu.VMEM((hops, rows, columns), F32),
            pltpu.VMEM((CHUNKS, 4 * piece, LANES), BF16),
            pltpu.VMEM((4 * piece, 4 * piece), BF16),
            pltpu.VMEM((2, tall, tall), BF16),
            pltpu.VMEM((tall, tall), BF16),
            pltpu.SemaphoreType.DMA((CHUNKS, hops)),
            pltpu.SemaphoreType.DMA((CHUNKS, hops)),
            pltpu.SemaphoreType.DMA((3,)),
            pltpu.SemaphoreType.DMA((3,)),
            pltpu.SemaphoreType.REGULAR((CHIPS_X // 2 + CHIPS_Z // 2 - 1,)),
        ],
        compiler_params=pltpu.CompilerParams(
            collective_id=0, has_side_effects=True, vmem_limit_bytes=60 * 1024 * 1024
        ),
        name="exchange",
    )(*operands)
    gradient = gradient.astype(F32)
    first_new = BETA_FIRST * first_old.astype(F32) + (1.0 - BETA_FIRST) * gradient
    second_new = BETA_SECOND * second_old.astype(F32) + (1.0 - BETA_SECOND) * gradient * gradient
    weight_old = weight_old.astype(F32)
    update = (
        first_new / CORRECT_FIRST / (jnp.sqrt(second_new / CORRECT_SECOND) + EPSILON)
        + DECAY_RATE * weight_old
    )
    weight_new = (weight_old - LEARNING_RATE * update).astype(BF16)
    return weight_new, first_new, second_new


def solution(mesh):
    return jax.shard_map(
        local,
        mesh=mesh,
        in_specs=(
            P(None, "node", "local"),
            P(None, "node", "local"),
            P(None, "node", "local"),
            P("node", "local", None, None),
            P("node", "local", None, None),
            P(),
            P(),
            P(),
            P(),
        ),
        out_specs=(P("node", None, "local"), P("node", None, "local"), P("node", None, "local")),
        check_vma=False,
    )
```

```python
import functools

import jax
import jax.numpy as jnp
from jax import lax
from jax.experimental import pallas as pl
from jax.experimental.pallas import tpu as pltpu
from jax.sharding import PartitionSpec as P

BETA_FIRST = 0.9
BETA_SECOND = 0.95
LEARNING_RATE = 0.1
DECAY_RATE = 0.1
EPSILON = 1e-08
CORRECT_FIRST = 1.0 - 0.9**10
CORRECT_SECOND = 1.0 - 0.95**10

MESH = pl.DeviceIdType.MESH
LANES = 128
CHUNKS = 4
CHIPS_X, CHIPS_Z = 4, 8
F32 = jnp.float32
BF16 = jnp.bfloat16


def dot(a, b):
    return jnp.dot(a, b, preferred_element_type=F32)


def dot_nt(a, b):
    return lax.dot_general(a, b, (((1,), (1,)), ((), ())), preferred_element_type=F32)


def equal(a, b):
    return jnp.where(a == b, 1.0, 0.0)


def iota(shape, axis):
    return lax.broadcasted_iota(jnp.int32, shape, axis)


def exchange(
    nodes,
    ring,
    old_place_hbm,
    new_place_hbm,
    old_owner_hbm,
    new_owner_hbm,
    weight_hbm,
    first_hbm,
    second_hbm,
    features_hbm,
    grad_hbm,
    out_weight,
    out_first,
    out_second,
    out_grad,
    old_place_ref,
    new_place_ref,
    old_owner_ref,
    new_owner_ref,
    weight_ref,
    first_ref,
    second_ref,
    features_ref,
    grad_ref,
    load_sem,
    block_sem,
    store_sem,
    ready,
    turned,
    ring_send,
    ring_recv,
    state_send,
    state_recv,
    rows_send,
    rows_recv,
    slots_send,
    slots_recv,
    parts,
    total,
    piece_order,
    order,
    match,
    ring_out_sem,
    ring_in_sem,
    out_sem,
    in_sem,
    round_sem,
):
    node = lax.axis_index("node")
    place = lax.axis_index("local")
    experts = weight_ref.shape[0] // 4
    rows = features_ref.shape[2]
    columns = 2 * LANES
    tall = 8 * nodes
    half = ring // 2
    loads = [
        pltpu.make_async_copy(source, target, load_sem.at[i])
        for i, (source, target) in enumerate(
            (
                (features_hbm, features_ref),
                (new_place_hbm, new_place_ref),
                (new_owner_hbm, new_owner_ref),
                (weight_hbm, weight_ref),
                (first_hbm, first_ref),
                (second_hbm, second_ref),
                (old_place_hbm, old_place_ref),
                (old_owner_hbm, old_owner_ref),
            )
        )
    ]

    x, z, core = node // (2 * CHIPS_Z), lax.rem(node // 2, CHIPS_Z), lax.rem(node, 2)

    def away(dx, dz, dc):
        to_x = lax.rem(x + dx, CHIPS_X) if dx else x
        to_z = lax.rem(z + dz, CHIPS_Z) if dz else z
        return (to_x * CHIPS_Z + to_z) * 2 + (1 - core if dc else core)

    def distance(offset):
        dx, dz = offset[0], offset[1]
        return min(dx, CHIPS_X - dx) + min(dz, CHIPS_Z - dz)

    offsets = [(dx, dz, dc) for dx in range(CHIPS_X) for dz in range(CHIPS_Z) for dc in range(2)][1:]
    offsets.sort(key=distance, reverse=True)
    farthest = distance(offsets[0])
    next_to = [(1, 0), (CHIPS_X - 1, 0), (0, 1), (0, CHIPS_Z - 1)]

    barrier = pltpu.get_barrier_semaphore()
    right = lax.rem(place + 1, ring)
    left = lax.rem(place + ring - 1, ring)
    for neighbour in (right, left):
        pl.semaphore_signal(barrier, inc=1, device_id=(node, neighbour), device_id_type=MESH)
    close = [(0, 0, 1)] + [(dx, dz, dc) for dx, dz in next_to for dc in range(2)]
    for offset in close:
        pl.semaphore_signal(barrier, inc=1, device_id=(away(*offset), place), device_id_type=MESH)

    def tell(r):
        for dx, dz in next_to:
            pl.semaphore_signal(
                round_sem.at[r - 1], inc=1, device_id=(away(dx, dz, 0), place), device_id_type=MESH
            )

    def hear(r):
        pl.semaphore_wait(round_sem.at[r - 1], len(next_to))

    chains = {(0, 1): half, (1, -1): half, (0, -1): half - 1, (1, 1): half - 1}
    slot = {}
    for k in range(half):
        for key, length in chains.items():
            if k < length:
                slot[key + (k,)] = len(slot)
    long = [key for key in chains if chains[key] == half]
    short = [key for key in chains if chains[key] < half]
    piece = rows // CHUNKS

    def columns_ahead(ahead):
        block = lax.rem(place + ahead + ring, ring)
        return pl.ds(pl.multiple_of(block * columns, columns), columns)

    needs = [(c, way * (chains[(c, way)] - k)) for c, way, k in slot] + [(0, 0), (1, 0)]
    blocks = {}
    for i, (c, ahead) in enumerate(needs):
        at = columns_ahead(ahead)
        blocks[(c, ahead)] = pltpu.make_async_copy(
            grad_hbm.at[c, :, at], grad_ref.at[c, :, at], block_sem.at[i]
        )
    loads[0].start()
    for need in needs[: len(chains)]:
        blocks[need].start()
    for load in loads[1:]:
        load.start()
    for need in needs[len(chains) :]:
        blocks[need].start()
    loads[0].wait()
    for c in range(2):
        turned[c] = features_ref[c].astype(F32).T.astype(BF16)

    def partial(c, ahead):
        blocks[(c, ahead)].wait()
        return dot(turned[c], grad_ref[c, :, columns_ahead(ahead)])

    def pieces(c, way, k):
        return CHUNKS

    def hop(c, way, k, j=0):
        at = slot[(c, way, k)]
        some = pl.ds(j * piece, rows // pieces(c, way, k))
        return pltpu.make_async_remote_copy(
            src_ref=ring_send.at[at, some],
            dst_ref=ring_recv.at[at, some],
            send_sem=ring_out_sem.at[at, j],
            recv_sem=ring_in_sem.at[at, j],
            device_id=(node, right if way == 1 else left),
            device_id_type=MESH,
        )

    def advance(c, way, k, j):
        at, before, some = slot[(c, way, k)], slot[(c, way, k - 1)], pl.ds(j * piece, piece)
        hop(c, way, k - 1, j).wait_recv()
        ring_send[at, some] = (parts[at, some] + ring_recv[before, some].astype(F32)).astype(BF16)
        hop(c, way, k, j).start()

    for c, way in chains:
        ring_send[slot[(c, way, 0)]] = partial(c, way * chains[(c, way)]).astype(BF16)
    pl.semaphore_wait(barrier, 2 + len(close))
    for j in range(CHUNKS):
        for c, way in chains:
            hop(c, way, 0, j).start()
    tell(1)
    for (c, way, k), at in slot.items():
        if k:
            parts[at] = partial(c, way * (chains[(c, way)] - k))
    for c in range(2):
        parts[slot[(c, 1, 0)]] = partial(c, 0)

    def scatter(send, recv, which, some):
        for offset in some:
            other = away(*offset)
            pltpu.make_async_remote_copy(
                src_ref=send.at[other],
                dst_ref=recv.at[node],
                send_sem=out_sem.at[which],
                recv_sem=in_sem.at[which],
                device_id=(other, place),
                device_id_type=MESH,
            ).start()

    def state_up_to(low, high):
        scatter(state_send, state_recv, 0, [o for o in offsets if low <= distance(o) <= high])

    def all_but_one(send, recv, which):
        return pltpu.make_async_remote_copy(
            src_ref=send.at[pl.ds(0, nodes - 1)],
            dst_ref=recv.at[pl.ds(0, nodes - 1)],
            send_sem=out_sem.at[which],
            recv_sem=in_sem.at[which],
            device_id=(lax.rem(node + 1, nodes), place),
            device_id_type=MESH,
        )

    for load in loads[1:]:
        load.wait()
    redundant = old_owner_ref.shape[1]
    slots = experts + redundant
    position = iota((tall, slots), 0) // 4

    def expert_of_slot(owner, repeat):
        owned = equal(iota((experts * repeat, redundant), 0) // repeat, owner).astype(BF16)
        tail = equal(iota((redundant, slots), 0) + experts, iota((redundant, slots), 1)).astype(BF16)
        primary = equal(iota((experts * repeat, slots), 0) // repeat, iota((experts * repeat, slots), 1))
        return (dot(owned, tail) + primary).astype(BF16)

    at_new = equal(position, new_place_ref[...]).astype(BF16)
    choose = dot_nt(at_new, expert_of_slot(new_owner_ref[...], 4))
    same = (iota((tall, 4 * experts), 0) % 4) == (iota((tall, 4 * experts), 1) % 4)
    choose = jnp.where(same, choose, 0.0).astype(BF16)
    for a, ref in enumerate((weight_ref, first_ref, second_ref)):
        picked = dot(choose, ref[...].astype(BF16))
        state_send[:, a] = picked.reshape(nodes, 8, LANES).astype(BF16)
    state_recv[node] = state_send[node]
    state_up_to(0, 1)
    heard = 0

    def listen(heard):
        if heard == farthest - 1:
            return heard
        heard += 1
        hear(heard)
        if heard < farthest - 1:
            tell(heard + 1)
        state_up_to(heard + 1, heard + 1)
        return heard

    for k in range(1, half):
        for j in range(CHUNKS):
            for c, way in chains:
                if k < chains[(c, way)]:
                    advance(c, way, k, j)
            due = ((k - 1) * CHUNKS + j + 1) * (farthest - 1) // ((half - 1) * CHUNKS)
            while heard < due:
                heard = listen(heard)
        if k == 1:
            at_old = equal(position, old_place_ref[...]).astype(BF16)
            held_new = dot_nt(at_new, expert_of_slot(new_owner_ref[...], 1)).astype(BF16)
            held_old = dot_nt(at_old, expert_of_slot(old_owner_ref[...], 1)).astype(BF16)
            pairs = dot_nt(held_new, held_old)
            tall_row, tall_column = iota((tall, tall), 0), iota((tall, tall), 1)
            match[...] = jnp.where((tall_row % 4) == (tall_column % 4), pairs, 0.0).astype(BF16)
        if k == 2:
            q, r = tall_row // rows, tall_row % rows
            order[0] = equal(tall_column, (r // 2) * 8 + q * 2 + r % 2).astype(BF16)
            owner = (r % piece) // 2 * CHUNKS + r // piece
            order[1] = equal(tall_column, owner * 8 + q * 2 + r % 2).astype(BF16)
            low = 4 * piece
            low_row, low_column = iota((low, low), 0), iota((low, low), 1)
            q, r = low_column // piece, low_column % piece
            piece_order[...] = equal(low_row, (r // 2) * 8 + q * 2 + r % 2).astype(BF16)

    group = nodes // CHUNKS
    line = group // CHIPS_X
    steps = sorted(
        range(group),
        key=lambda k: -distance((k // line, k % line * CHIPS_Z // line)),
    )
    hosts = [
        (
            k,
            lax.rem(node // (line * CHUNKS) + k // line, CHIPS_X) * line
            + lax.rem(node // CHUNKS + k % line, line),
        )
        for k in steps
    ]
    for j in range(CHUNKS):
        for c in range(2):
            value = parts[slot[(c, 1, 0)], pl.ds(j * piece, piece), :]
            for way in (1, -1):
                k = chains[(c, way)] - 1
                hop(c, way, k, j).wait_recv()
                value = value + ring_recv[slot[(c, way, k)], pl.ds(j * piece, piece), :].astype(F32)
            value = value.astype(BF16)
            for h in range(2):
                total[j, pl.ds((2 * c + h) * piece, piece), :] = value[:, h * LANES : (h + 1) * LANES]
        mine = dot(piece_order[...], total[j])
        rows_send[j] = mine.reshape(group, 8, LANES).astype(BF16)

        for step, at in hosts:
            copy = pltpu.make_async_remote_copy(
                src_ref=rows_send.at[j, at],
                dst_ref=rows_recv.at[node],
                send_sem=out_sem.at[1],
                recv_sem=in_sem.at[1],
                device_id=(at * CHUNKS + j, place),
                device_id_type=MESH,
            )
            if step:
                copy.start()
            else:
                pl.when(lax.rem(node, CHUNKS) != j)(copy.start)

    rows_recv[node] = rows_send[lax.rem(node, CHUNKS), node // CHUNKS]

    outs = (out_weight, out_first, out_second, out_grad)
    stores = [pltpu.make_async_copy(ready.at[a], outs[a], store_sem.at[a]) for a in range(4)]

    def natural(block, a):
        value = dot(order[a // 3], block.astype(F32).reshape(tall, LANES).astype(BF16))
        for c in range(2):
            for h in range(2):
                outs[a][c, :, h * LANES : (h + 1) * LANES] = value[
                    (2 * c + h) * rows : (2 * c + h + 1) * rows
                ].astype(BF16)

    all_but_one(state_send, state_recv, 0).wait_recv()
    for a in range(3):
        natural(state_recv[:, a], a)

    all_but_one(rows_recv, rows_recv, 1).wait_recv()
    owned = rows_recv[...].astype(F32).reshape(tall, LANES).astype(BF16)
    stretch = nodes // CHIPS_X
    for dx in sorted(range(CHIPS_X), key=lambda dx: -min(dx, CHIPS_X - dx)):
        to_x = lax.rem(x + dx, CHIPS_X)
        at = pl.multiple_of(to_x * (8 * stretch), 8 * stretch)
        summed = dot(match[pl.ds(at, 8 * stretch), :], owned)
        slots_send[pl.ds(to_x * stretch, stretch)] = summed.reshape(stretch, 8, LANES).astype(BF16)
        scatter(slots_send, slots_recv, 2, [o for o in offsets if o[0] == dx])
    slots_recv[node] = slots_send[node]

    for key, length in chains.items():
        for k in range(length):
            for j in range(pieces(*key, k)):
                hop(*key, k, j).wait_send()
    all_but_one(state_send, state_recv, 0).wait_send()
    all_but_one(rows_recv, rows_recv, 1).wait_send()
    all_but_one(slots_send, slots_recv, 2).wait_recv()
    natural(slots_recv[...], 3)
    all_but_one(slots_send, slots_recv, 2).wait_send()


def by_row(state):
    experts = state.shape[0]
    return state.reshape(experts, 2, 2, LANES).transpose(0, 2, 1, 3).reshape(4 * experts, LANES)


def local(
    master_weight,
    first_moment,
    second_moment,
    features,
    grad_out,
    old_place,
    new_place,
    old_owner,
    new_owner,
):
    nodes, ring = lax.axis_size("node"), lax.axis_size("local")
    experts = master_weight.shape[0]
    rows = features.shape[3]
    columns = master_weight.shape[2]
    tall = 8 * nodes
    hops = 2 * (ring - 1)
    piece = rows // CHUNKS
    operands = (
        old_place.reshape(1, -1),
        new_place.reshape(1, -1),
        old_owner.reshape(1, -1),
        new_owner.reshape(1, -1),
        by_row(master_weight),
        by_row(first_moment),
        by_row(second_moment),
        features.reshape(2, features.shape[2], rows),
        grad_out.reshape(2, grad_out.shape[2], grad_out.shape[3]),
    )
    hbm = pl.BlockSpec(memory_space=pltpu.HBM)
    operands = tuple(pltpu.with_memory_space_constraint(x, pltpu.HBM) for x in operands)
    block = pltpu.VMEM((2, rows, columns), BF16)
    weight_old, first_old, second_old, gradient = pl.pallas_call(
        functools.partial(exchange, nodes, ring),
        out_shape=(block,) * 4,
        in_specs=[hbm] * len(operands),
        out_specs=(pl.BlockSpec(memory_space=pltpu.VMEM),) * 4,
        scratch_shapes=[
            *(pltpu.VMEM(operand.shape, operand.dtype) for operand in operands),
            pltpu.SemaphoreType.DMA((len(operands),)),
            pltpu.SemaphoreType.DMA((hops + 2,)),
            pltpu.SemaphoreType.DMA((4,)),
            pltpu.VMEM((4, 2, rows, columns), BF16),
            pltpu.VMEM((2, rows, features.shape[2]), BF16),
            pltpu.VMEM((hops, rows, columns), BF16),
            pltpu.VMEM((hops, rows, columns), BF16),
            pltpu.VMEM((nodes, 3, 8, LANES), BF16),
            pltpu.VMEM((nodes, 3, 8, LANES), BF16),
            pltpu.VMEM((CHUNKS, nodes // CHUNKS, 8, LANES), BF16),
            pltpu.VMEM((nodes, 8, LANES), BF16),
            pltpu.VMEM((nodes, 8, LANES), BF16),
            pltpu.VMEM((nodes, 8, LANES), BF16),
            pltpu.VMEM((hops, rows, columns), F32),
            pltpu.VMEM((CHUNKS, 4 * piece, LANES), BF16),
            pltpu.VMEM((4 * piece, 4 * piece), BF16),
            pltpu.VMEM((2, tall, tall), BF16),
            pltpu.VMEM((tall, tall), BF16),
            pltpu.SemaphoreType.DMA((hops, CHUNKS)),
            pltpu.SemaphoreType.DMA((hops, CHUNKS)),
            pltpu.SemaphoreType.DMA((3,)),
            pltpu.SemaphoreType.DMA((3,)),
            pltpu.SemaphoreType.REGULAR((CHIPS_X // 2 + CHIPS_Z // 2 - 1,)),
        ],
        compiler_params=pltpu.CompilerParams(
            collective_id=0, has_side_effects=True, vmem_limit_bytes=40 * 1024 * 1024
        ),
        name="exchange",
    )(*operands)
    gradient = gradient.astype(F32)
    first_new = BETA_FIRST * first_old.astype(F32) + (1.0 - BETA_FIRST) * gradient
    second_new = BETA_SECOND * second_old.astype(F32) + (1.0 - BETA_SECOND) * gradient * gradient
    weight_old = weight_old.astype(F32)
    update = (
        first_new / CORRECT_FIRST / (jnp.sqrt(second_new / CORRECT_SECOND) + EPSILON)
        + DECAY_RATE * weight_old
    )
    weight_new = (weight_old - LEARNING_RATE * update).astype(BF16)
    return weight_new, first_new, second_new


def solution(mesh):
    return jax.shard_map(
        local,
        mesh=mesh,
        in_specs=(
            P(None, "node", "local"),
            P(None, "node", "local"),
            P(None, "node", "local"),
            P("node", "local", None, None),
            P("node", "local", None, None),
            P(),
            P(),
            P(),
            P(),
        ),
        out_specs=(P("node", None, "local"), P("node", None, "local"), P("node", None, "local")),
        check_vma=False,
    )
```

```python
import functools

import jax
import jax.numpy as jnp
from jax import lax
from jax.experimental import pallas as pl
from jax.experimental.pallas import tpu as pltpu
from jax.sharding import PartitionSpec as P

BETA_FIRST = 0.9
BETA_SECOND = 0.95
LEARNING_RATE = 0.1
DECAY_RATE = 0.1
EPSILON = 1e-08
CORRECT_FIRST = 1.0 - 0.9**10
CORRECT_SECOND = 1.0 - 0.95**10

MESH = pl.DeviceIdType.MESH
LANES = 128
CHUNKS = 4
CHIPS_X, CHIPS_Z = 4, 8
F32 = jnp.float32
BF16 = jnp.bfloat16


def dot(a, b):
    return jnp.dot(a, b, preferred_element_type=F32)


def dot_nt(a, b):
    return lax.dot_general(a, b, (((1,), (1,)), ((), ())), preferred_element_type=F32)


def equal(a, b):
    return jnp.where(a == b, 1.0, 0.0)


def iota(shape, axis):
    return lax.broadcasted_iota(jnp.int32, shape, axis)


def exchange(
    nodes,
    ring,
    old_place_hbm,
    new_place_hbm,
    old_owner_hbm,
    new_owner_hbm,
    weight_hbm,
    first_hbm,
    second_hbm,
    features_hbm,
    grad_hbm,
    out_weight,
    out_first,
    out_second,
    out_grad,
    old_place_ref,
    new_place_ref,
    old_owner_ref,
    new_owner_ref,
    weight_ref,
    first_ref,
    second_ref,
    features_ref,
    grad_ref,
    load_sem,
    block_sem,
    turned,
    ring_send,
    ring_recv,
    state_send,
    state_recv,
    rows_send,
    rows_recv,
    slots_send,
    slots_recv,
    parts,
    total,
    piece_order,
    order,
    match,
    ring_out_sem,
    ring_in_sem,
    out_sem,
    in_sem,
    round_sem,
):
    node = lax.axis_index("node")
    place = lax.axis_index("local")
    experts = weight_ref.shape[0] // 4
    rows = features_ref.shape[2]
    columns = 2 * LANES
    tall = 8 * nodes
    half = ring // 2
    loads = [
        pltpu.make_async_copy(source, target, load_sem.at[i])
        for i, (source, target) in enumerate(
            (
                (features_hbm, features_ref),
                (new_place_hbm, new_place_ref),
                (new_owner_hbm, new_owner_ref),
                (weight_hbm, weight_ref),
                (first_hbm, first_ref),
                (second_hbm, second_ref),
                (old_place_hbm, old_place_ref),
                (old_owner_hbm, old_owner_ref),
            )
        )
    ]

    x, z, core = node // (2 * CHIPS_Z), lax.rem(node // 2, CHIPS_Z), lax.rem(node, 2)

    def away(dx, dz, dc):
        to_x = lax.rem(x + dx, CHIPS_X) if dx else x
        to_z = lax.rem(z + dz, CHIPS_Z) if dz else z
        return (to_x * CHIPS_Z + to_z) * 2 + (1 - core if dc else core)

    def distance(offset):
        dx, dz = offset[0], offset[1]
        return min(dx, CHIPS_X - dx) + min(dz, CHIPS_Z - dz)

    offsets = [(dx, dz, dc) for dx in range(CHIPS_X) for dz in range(CHIPS_Z) for dc in range(2)][1:]
    offsets.sort(key=distance, reverse=True)
    farthest = distance(offsets[0])
    next_to = [(1, 0), (CHIPS_X - 1, 0), (0, 1), (0, CHIPS_Z - 1)]

    barrier = pltpu.get_barrier_semaphore()
    right = lax.rem(place + 1, ring)
    left = lax.rem(place + ring - 1, ring)
    right_two = lax.rem(place + 2, ring)
    left_two = lax.rem(place + ring - 2, ring)
    for neighbour in (right, left, right_two, left_two):
        pl.semaphore_signal(barrier, inc=1, device_id=(node, neighbour), device_id_type=MESH)
    close = [(0, 0, 1)] + [(dx, dz, dc) for dx, dz in next_to for dc in range(2)]
    for offset in close:
        pl.semaphore_signal(barrier, inc=1, device_id=(away(*offset), place), device_id_type=MESH)

    def tell(r):
        for dx, dz in next_to:
            pl.semaphore_signal(
                round_sem.at[r - 1], inc=1, device_id=(away(dx, dz, 0), place), device_id_type=MESH
            )

    def hear(r):
        pl.semaphore_wait(round_sem.at[r - 1], len(next_to))

    chains = {(0, 1): half, (1, -1): half, (0, -1): half - 1, (1, 1): half - 1}
    slot = {}
    for k in range(half):
        for key, length in chains.items():
            if k < length:
                slot[key + (k,)] = len(slot)
    long = [key for key in chains if chains[key] == half]
    short = [key for key in chains if chains[key] < half]
    piece = rows // CHUNKS

    def columns_ahead(ahead):
        block = lax.rem(place + ahead + ring, ring)
        return pl.ds(pl.multiple_of(block * columns, columns), columns)

    needs = [(c, way * (chains[(c, way)] - k)) for c, way, k in slot] + [(0, 0), (1, 0)]
    blocks = {}
    for i, (c, ahead) in enumerate(needs):
        at = columns_ahead(ahead)
        blocks[(c, ahead)] = pltpu.make_async_copy(
            grad_hbm.at[c, :, at], grad_ref.at[c, :, at], block_sem.at[i]
        )
    loads[0].start()
    for need in needs[: len(chains)]:
        blocks[need].start()
    for load in loads[1:]:
        load.start()
    for need in needs[len(chains) :]:
        blocks[need].start()
    loads[0].wait()
    for c in range(2):
        turned[c] = features_ref[c].astype(F32).T.astype(BF16)

    def partial(c, ahead):
        blocks[(c, ahead)].wait()
        return dot(turned[c], grad_ref[c, :, columns_ahead(ahead)])

    def hop(c, way, k, j=0):
        at = slot[(c, way, k)]
        if (c, way) in long and k == half - 2:
            to = right_two if way == 1 else left_two
        else:
            to = right if way == 1 else left
        some = pl.ds(j * piece, piece)
        return pltpu.make_async_remote_copy(
            src_ref=ring_send.at[at, some],
            dst_ref=ring_recv.at[at, some],
            send_sem=ring_out_sem.at[at, j],
            recv_sem=ring_in_sem.at[at, j],
            device_id=(node, to),
            device_id_type=MESH,
        )

    def advance(c, way, k, j):
        at, before, some = slot[(c, way, k)], slot[(c, way, k - 1)], pl.ds(j * piece, piece)
        hop(c, way, k - 1, j).wait_recv()
        ring_send[at, some] = (parts[at, some] + ring_recv[before, some].astype(F32)).astype(BF16)
        hop(c, way, k, j).start()

    for c, way in chains:
        ring_send[slot[(c, way, 0)]] = partial(c, way * chains[(c, way)]).astype(BF16)
    pl.semaphore_wait(barrier, 4 + len(close))
    for j in range(CHUNKS):
        for c, way in chains:
            hop(c, way, 0, j).start()
    tell(1)
    for (c, way, k), at in slot.items():
        if k == half - 1:
            ring_send[at] = partial(c, way).astype(BF16)
        elif k:
            parts[at] = partial(c, way * (chains[(c, way)] - k))
    for c in range(2):
        parts[slot[(c, 1, 0)]] = partial(c, 0)

    def scatter(send, recv, which, some):
        for offset in some:
            other = away(*offset)
            pltpu.make_async_remote_copy(
                src_ref=send.at[other],
                dst_ref=recv.at[node],
                send_sem=out_sem.at[which],
                recv_sem=in_sem.at[which],
                device_id=(other, place),
                device_id_type=MESH,
            ).start()

    def state_up_to(low, high):
        scatter(state_send, state_recv, 0, [o for o in offsets if low <= distance(o) <= high])

    def all_but_one(send, recv, which):
        return pltpu.make_async_remote_copy(
            src_ref=send.at[pl.ds(0, nodes - 1)],
            dst_ref=recv.at[pl.ds(0, nodes - 1)],
            send_sem=out_sem.at[which],
            recv_sem=in_sem.at[which],
            device_id=(lax.rem(node + 1, nodes), place),
            device_id_type=MESH,
        )

    for load in loads[1:]:
        load.wait()
    redundant = old_owner_ref.shape[1]
    slots = experts + redundant
    position = iota((tall, slots), 0) // 4

    def expert_of_slot(owner, repeat):
        owned = equal(iota((experts * repeat, redundant), 0) // repeat, owner).astype(BF16)
        tail = equal(iota((redundant, slots), 0) + experts, iota((redundant, slots), 1)).astype(BF16)
        primary = equal(iota((experts * repeat, slots), 0) // repeat, iota((experts * repeat, slots), 1))
        return (dot(owned, tail) + primary).astype(BF16)

    at_new = equal(position, new_place_ref[...]).astype(BF16)
    choose = dot_nt(at_new, expert_of_slot(new_owner_ref[...], 4))
    same = (iota((tall, 4 * experts), 0) % 4) == (iota((tall, 4 * experts), 1) % 4)
    choose = jnp.where(same, choose, 0.0).astype(BF16)
    for a, ref in enumerate((weight_ref, first_ref, second_ref)):
        picked = dot(choose, ref[...].astype(BF16))
        state_send[:, a] = picked.reshape(nodes, 8, LANES).astype(BF16)
    state_recv[node] = state_send[node]
    state_up_to(0, 1)
    heard = 0

    def listen(heard):
        if heard == farthest - 1:
            return heard
        heard += 1
        hear(heard)
        if heard < farthest - 1:
            tell(heard + 1)
        state_up_to(heard + 1, heard + 1)
        return heard

    for k in range(1, half - 1):
        for j in range(CHUNKS):
            for c, way in chains:
                advance(c, way, k, j)
            if k == half - 2:
                for c, way in long:
                    hop(c, way, half - 1, j).start()
            due = ((k - 1) * CHUNKS + j + 1) * (farthest - 1) // ((half - 2) * CHUNKS)
            while heard < due:
                heard = listen(heard)
        if k == 1:
            at_old = equal(position, old_place_ref[...]).astype(BF16)
            held_new = dot_nt(at_new, expert_of_slot(new_owner_ref[...], 1)).astype(BF16)
            held_old = dot_nt(at_old, expert_of_slot(old_owner_ref[...], 1)).astype(BF16)
            pairs = dot_nt(held_new, held_old)
            tall_row, tall_column = iota((tall, tall), 0), iota((tall, tall), 1)
            match[...] = jnp.where((tall_row % 4) == (tall_column % 4), pairs, 0.0).astype(BF16)
        if k == 2:
            q, r = tall_row // rows, tall_row % rows
            order[0] = equal(tall_column, (r // 2) * 8 + q * 2 + r % 2).astype(BF16)
            owner = (r % piece) // 2 * CHUNKS + r // piece
            order[1] = equal(tall_column, owner * 8 + q * 2 + r % 2).astype(BF16)
            low = 4 * piece
            low_row, low_column = iota((low, low), 0), iota((low, low), 1)
            q, r = low_column // piece, low_column % piece
            piece_order[...] = equal(low_row, (r // 2) * 8 + q * 2 + r % 2).astype(BF16)

    group = nodes // CHUNKS
    line = group // CHIPS_X
    steps = sorted(
        range(group),
        key=lambda k: -distance((k // line, k % line * CHIPS_Z // line)),
    )
    hosts = [
        (
            k,
            lax.rem(node // (line * CHUNKS) + k // line, CHIPS_X) * line
            + lax.rem(node // CHUNKS + k % line, line),
        )
        for k in steps
    ]
    for j in range(CHUNKS):
        for c in range(2):
            value = parts[slot[(c, 1, 0)], pl.ds(j * piece, piece), :]
            for key in [(c, 1, half - 2), (c, -1, half - 2), (c, 1, half - 1), (c, -1, half - 1)]:
                if key in slot:
                    hop(*key, j).wait_recv()
                    value = value + ring_recv[slot[key], pl.ds(j * piece, piece), :].astype(F32)
            value = value.astype(BF16)
            for h in range(2):
                total[j, pl.ds((2 * c + h) * piece, piece), :] = value[:, h * LANES : (h + 1) * LANES]
        mine = dot(piece_order[...], total[j])
        rows_send[j] = mine.reshape(group, 8, LANES).astype(BF16)

        for step, at in hosts:
            copy = pltpu.make_async_remote_copy(
                src_ref=rows_send.at[j, at],
                dst_ref=rows_recv.at[node],
                send_sem=out_sem.at[1],
                recv_sem=in_sem.at[1],
                device_id=(at * CHUNKS + j, place),
                device_id_type=MESH,
            )
            if step:
                copy.start()
            else:
                pl.when(lax.rem(node, CHUNKS) != j)(copy.start)

    rows_recv[node] = rows_send[lax.rem(node, CHUNKS), node // CHUNKS]

    outs = (out_weight, out_first, out_second, out_grad)

    def natural(block, a):
        value = dot(order[a // 3], block.astype(F32).reshape(tall, LANES).astype(BF16))
        for c in range(2):
            for h in range(2):
                outs[a][c, :, h * LANES : (h + 1) * LANES] = value[
                    (2 * c + h) * rows : (2 * c + h + 1) * rows
                ].astype(BF16)

    all_but_one(state_send, state_recv, 0).wait_recv()
    for a in range(3):
        natural(state_recv[:, a], a)

    all_but_one(rows_recv, rows_recv, 1).wait_recv()
    owned = rows_recv[...].astype(F32).reshape(tall, LANES).astype(BF16)
    stretch = nodes // CHIPS_X
    for dx in sorted(range(CHIPS_X), key=lambda dx: -min(dx, CHIPS_X - dx)):
        to_x = lax.rem(x + dx, CHIPS_X)
        at = pl.multiple_of(to_x * (8 * stretch), 8 * stretch)
        summed = dot(match[pl.ds(at, 8 * stretch), :], owned)
        slots_send[pl.ds(to_x * stretch, stretch)] = summed.reshape(stretch, 8, LANES).astype(BF16)
        scatter(slots_send, slots_recv, 2, [o for o in offsets if o[0] == dx])
    slots_recv[node] = slots_send[node]

    for key, length in chains.items():
        for k in range(length):
            for j in range(CHUNKS):
                hop(*key, k, j).wait_send()
    all_but_one(state_send, state_recv, 0).wait_send()
    all_but_one(rows_recv, rows_recv, 1).wait_send()
    all_but_one(slots_send, slots_recv, 2).wait_recv()
    natural(slots_recv[...], 3)
    all_but_one(slots_send, slots_recv, 2).wait_send()


def by_row(state):
    experts = state.shape[0]
    return state.reshape(experts, 2, 2, LANES).transpose(0, 2, 1, 3).reshape(4 * experts, LANES)


def local(
    master_weight,
    first_moment,
    second_moment,
    features,
    grad_out,
    old_place,
    new_place,
    old_owner,
    new_owner,
):
    nodes, ring = lax.axis_size("node"), lax.axis_size("local")
    experts = master_weight.shape[0]
    rows = features.shape[3]
    columns = master_weight.shape[2]
    tall = 8 * nodes
    hops = 2 * (ring - 1)
    piece = rows // CHUNKS
    operands = (
        old_place.reshape(1, -1),
        new_place.reshape(1, -1),
        old_owner.reshape(1, -1),
        new_owner.reshape(1, -1),
        by_row(master_weight),
        by_row(first_moment),
        by_row(second_moment),
        features.reshape(2, features.shape[2], rows),
        grad_out.reshape(2, grad_out.shape[2], grad_out.shape[3]),
    )
    hbm = pl.BlockSpec(memory_space=pltpu.HBM)
    operands = tuple(pltpu.with_memory_space_constraint(x, pltpu.HBM) for x in operands)
    block = pltpu.VMEM((2, rows, columns), BF16)
    weight_old, first_old, second_old, gradient = pl.pallas_call(
        functools.partial(exchange, nodes, ring),
        out_shape=(block,) * 4,
        in_specs=[hbm] * len(operands),
        out_specs=(pl.BlockSpec(memory_space=pltpu.VMEM),) * 4,
        scratch_shapes=[
            *(pltpu.VMEM(operand.shape, operand.dtype) for operand in operands),
            pltpu.SemaphoreType.DMA((len(operands),)),
            pltpu.SemaphoreType.DMA((hops + 2,)),
            pltpu.VMEM((2, rows, features.shape[2]), BF16),
            pltpu.VMEM((hops, rows, columns), BF16),
            pltpu.VMEM((hops, rows, columns), BF16),
            pltpu.VMEM((nodes, 3, 8, LANES), BF16),
            pltpu.VMEM((nodes, 3, 8, LANES), BF16),
            pltpu.VMEM((CHUNKS, nodes // CHUNKS, 8, LANES), BF16),
            pltpu.VMEM((nodes, 8, LANES), BF16),
            pltpu.VMEM((nodes, 8, LANES), BF16),
            pltpu.VMEM((nodes, 8, LANES), BF16),
            pltpu.VMEM((hops, rows, columns), F32),
            pltpu.VMEM((CHUNKS, 4 * piece, LANES), BF16),
            pltpu.VMEM((4 * piece, 4 * piece), BF16),
            pltpu.VMEM((2, tall, tall), BF16),
            pltpu.VMEM((tall, tall), BF16),
            pltpu.SemaphoreType.DMA((hops, CHUNKS)),
            pltpu.SemaphoreType.DMA((hops, CHUNKS)),
            pltpu.SemaphoreType.DMA((3,)),
            pltpu.SemaphoreType.DMA((3,)),
            pltpu.SemaphoreType.REGULAR((CHIPS_X // 2 + CHIPS_Z // 2 - 1,)),
        ],
        compiler_params=pltpu.CompilerParams(
            collective_id=0, has_side_effects=True, vmem_limit_bytes=40 * 1024 * 1024
        ),
        name="exchange",
    )(*operands)
    gradient = gradient.astype(F32)
    first_new = BETA_FIRST * first_old.astype(F32) + (1.0 - BETA_FIRST) * gradient
    second_new = BETA_SECOND * second_old.astype(F32) + (1.0 - BETA_SECOND) * gradient * gradient
    weight_old = weight_old.astype(F32)
    update = (
        first_new / CORRECT_FIRST / (jnp.sqrt(second_new / CORRECT_SECOND) + EPSILON)
        + DECAY_RATE * weight_old
    )
    weight_new = (weight_old - LEARNING_RATE * update).astype(BF16)
    return weight_new, first_new, second_new


def solution(mesh):
    return jax.shard_map(
        local,
        mesh=mesh,
        in_specs=(
            P(None, "node", "local"),
            P(None, "node", "local"),
            P(None, "node", "local"),
            P("node", "local", None, None),
            P("node", "local", None, None),
            P(),
            P(),
            P(),
            P(),
        ),
        out_specs=(P("node", None, "local"), P("node", None, "local"), P("node", None, "local")),
        check_vma=False,
    )
```

```python
import functools

import jax
import jax.numpy as jnp
from jax import lax
from jax.experimental import pallas as pl
from jax.experimental.pallas import tpu as pltpu
from jax.sharding import PartitionSpec as P

BETA_FIRST = 0.9
BETA_SECOND = 0.95
LEARNING_RATE = 0.1
DECAY_RATE = 0.1
EPSILON = 1e-08
CORRECT_FIRST = 1.0 - 0.9**10
CORRECT_SECOND = 1.0 - 0.95**10

MESH = pl.DeviceIdType.MESH
LANES = 128
CHUNKS = 2
CHIPS_X, CHIPS_Z = 4, 8
F32 = jnp.float32
BF16 = jnp.bfloat16


def dot(a, b):
    return jnp.dot(a, b, preferred_element_type=F32)


def dot_nt(a, b):
    return lax.dot_general(a, b, (((1,), (1,)), ((), ())), preferred_element_type=F32)


def equal(a, b):
    return jnp.where(a == b, 1.0, 0.0)


def iota(shape, axis):
    return lax.broadcasted_iota(jnp.int32, shape, axis)


def exchange(
    nodes,
    ring,
    old_place_hbm,
    new_place_hbm,
    old_owner_hbm,
    new_owner_hbm,
    weight_hbm,
    first_hbm,
    second_hbm,
    features_hbm,
    grad_hbm,
    out_weight,
    out_first,
    out_second,
    out_grad,
    old_place_ref,
    new_place_ref,
    old_owner_ref,
    new_owner_ref,
    weight_ref,
    first_ref,
    second_ref,
    features_ref,
    grad_ref,
    load_sem,
    block_sem,
    turned,
    ring_send,
    ring_recv,
    state_send,
    state_recv,
    rows_send,
    rows_recv,
    slots_send,
    slots_recv,
    parts,
    total,
    piece_order,
    order,
    match,
    ring_out_sem,
    ring_in_sem,
    out_sem,
    in_sem,
    round_sem,
):
    node = lax.axis_index("node")
    place = lax.axis_index("local")
    experts = weight_ref.shape[0] // 4
    rows = features_ref.shape[2]
    columns = 2 * LANES
    tall = 8 * nodes
    half = ring // 2
    loads = [
        pltpu.make_async_copy(source, target, load_sem.at[i])
        for i, (source, target) in enumerate(
            (
                (features_hbm, features_ref),
                (new_place_hbm, new_place_ref),
                (new_owner_hbm, new_owner_ref),
                (weight_hbm, weight_ref),
                (first_hbm, first_ref),
                (second_hbm, second_ref),
                (old_place_hbm, old_place_ref),
                (old_owner_hbm, old_owner_ref),
            )
        )
    ]

    x, z, core = node // (2 * CHIPS_Z), lax.rem(node // 2, CHIPS_Z), lax.rem(node, 2)

    def away(dx, dz, dc):
        to_x = lax.rem(x + dx, CHIPS_X) if dx else x
        to_z = lax.rem(z + dz, CHIPS_Z) if dz else z
        return (to_x * CHIPS_Z + to_z) * 2 + (1 - core if dc else core)

    def distance(offset):
        dx, dz = offset[0], offset[1]
        return min(dx, CHIPS_X - dx) + min(dz, CHIPS_Z - dz)

    offsets = [(dx, dz, dc) for dx in range(CHIPS_X) for dz in range(CHIPS_Z) for dc in range(2)][1:]
    offsets.sort(key=distance, reverse=True)
    farthest = distance(offsets[0])
    next_to = [(1, 0), (CHIPS_X - 1, 0), (0, 1), (0, CHIPS_Z - 1)]

    barrier = pltpu.get_barrier_semaphore()
    right = lax.rem(place + 1, ring)
    left = lax.rem(place + ring - 1, ring)
    right_two = lax.rem(place + 2, ring)
    left_two = lax.rem(place + ring - 2, ring)
    for neighbour in (right, left, right_two, left_two):
        pl.semaphore_signal(barrier, inc=1, device_id=(node, neighbour), device_id_type=MESH)
    close = [(0, 0, 1)] + [(dx, dz, dc) for dx, dz in next_to for dc in range(2)]
    for offset in close:
        pl.semaphore_signal(barrier, inc=1, device_id=(away(*offset), place), device_id_type=MESH)

    def tell(r):
        for dx, dz in next_to:
            pl.semaphore_signal(
                round_sem.at[r - 1], inc=1, device_id=(away(dx, dz, 0), place), device_id_type=MESH
            )

    def hear(r):
        pl.semaphore_wait(round_sem.at[r - 1], len(next_to))

    chains = {(0, 1): half, (1, -1): half, (0, -1): half - 1, (1, 1): half - 1}
    slot = {}
    for k in range(half):
        for key, length in chains.items():
            if k < length:
                slot[key + (k,)] = len(slot)
    long = [key for key in chains if chains[key] == half]
    short = [key for key in chains if chains[key] < half]
    piece = rows // CHUNKS

    def columns_ahead(ahead):
        block = lax.rem(place + ahead + ring, ring)
        return pl.ds(pl.multiple_of(block * columns, columns), columns)

    needs = [(c, way * (chains[(c, way)] - k)) for c, way, k in slot] + [(0, 0), (1, 0)]
    blocks = {}
    for i, (c, ahead) in enumerate(needs):
        at = columns_ahead(ahead)
        blocks[(c, ahead)] = pltpu.make_async_copy(
            grad_hbm.at[c, :, at], grad_ref.at[c, :, at], block_sem.at[i]
        )
    loads[0].start()
    for need in needs[: len(chains)]:
        blocks[need].start()
    for load in loads[1:]:
        load.start()
    for need in needs[len(chains) :]:
        blocks[need].start()
    loads[0].wait()
    for c in range(2):
        turned[c] = features_ref[c].astype(F32).T.astype(BF16)

    def partial(c, ahead):
        blocks[(c, ahead)].wait()
        return dot(turned[c], grad_ref[c, :, columns_ahead(ahead)])

    def hop(c, way, k, j=0):
        at = slot[(c, way, k)]
        if (c, way) in long and k == half - 2:
            to = right_two if way == 1 else left_two
        else:
            to = right if way == 1 else left
        some = pl.ds(j * piece, piece)
        return pltpu.make_async_remote_copy(
            src_ref=ring_send.at[at, some],
            dst_ref=ring_recv.at[at, some],
            send_sem=ring_out_sem.at[at, j],
            recv_sem=ring_in_sem.at[at, j],
            device_id=(node, to),
            device_id_type=MESH,
        )

    def advance(c, way, k, j):
        at, before, some = slot[(c, way, k)], slot[(c, way, k - 1)], pl.ds(j * piece, piece)
        hop(c, way, k - 1, j).wait_recv()
        ring_send[at, some] = (parts[at, some] + ring_recv[before, some].astype(F32)).astype(BF16)
        hop(c, way, k, j).start()

    for c, way in chains:
        ring_send[slot[(c, way, 0)]] = partial(c, way * chains[(c, way)]).astype(BF16)
    pl.semaphore_wait(barrier, 4 + len(close))
    for j in range(CHUNKS):
        for c, way in chains:
            hop(c, way, 0, j).start()
    tell(1)
    for (c, way, k), at in slot.items():
        if k == half - 1:
            ring_send[at] = partial(c, way).astype(BF16)
        elif k:
            parts[at] = partial(c, way * (chains[(c, way)] - k))
    for c in range(2):
        parts[slot[(c, 1, 0)]] = partial(c, 0)

    def scatter(send, recv, which, some):
        for offset in some:
            other = away(*offset)
            pltpu.make_async_remote_copy(
                src_ref=send.at[other],
                dst_ref=recv.at[node],
                send_sem=out_sem.at[which],
                recv_sem=in_sem.at[which],
                device_id=(other, place),
                device_id_type=MESH,
            ).start()

    def state_up_to(low, high):
        scatter(state_send, state_recv, 0, [o for o in offsets if low <= distance(o) <= high])

    def all_but_one(send, recv, which):
        return pltpu.make_async_remote_copy(
            src_ref=send.at[pl.ds(0, nodes - 1)],
            dst_ref=recv.at[pl.ds(0, nodes - 1)],
            send_sem=out_sem.at[which],
            recv_sem=in_sem.at[which],
            device_id=(lax.rem(node + 1, nodes), place),
            device_id_type=MESH,
        )

    for load in loads[1:]:
        load.wait()
    redundant = old_owner_ref.shape[1]
    slots = experts + redundant
    position = iota((tall, slots), 0) // 4

    def expert_of_slot(owner, repeat):
        owned = equal(iota((experts * repeat, redundant), 0) // repeat, owner).astype(BF16)
        tail = equal(iota((redundant, slots), 0) + experts, iota((redundant, slots), 1)).astype(BF16)
        primary = equal(iota((experts * repeat, slots), 0) // repeat, iota((experts * repeat, slots), 1))
        return (dot(owned, tail) + primary).astype(BF16)

    at_new = equal(position, new_place_ref[...]).astype(BF16)
    choose = dot_nt(at_new, expert_of_slot(new_owner_ref[...], 4))
    same = (iota((tall, 4 * experts), 0) % 4) == (iota((tall, 4 * experts), 1) % 4)
    choose = jnp.where(same, choose, 0.0).astype(BF16)
    for a, ref in enumerate((weight_ref, first_ref, second_ref)):
        picked = dot(choose, ref[...].astype(BF16))
        state_send[:, a] = picked.reshape(nodes, 8, LANES).astype(BF16)
    state_recv[node] = state_send[node]
    state_up_to(0, 1)
    heard = 0

    def listen(heard):
        if heard == farthest - 1:
            return heard
        heard += 1
        hear(heard)
        if heard < farthest - 1:
            tell(heard + 1)
        state_up_to(heard + 1, heard + 1)
        return heard

    heard = listen(heard)
    for k in range(1, half - 1):
        for j in range(CHUNKS):
            for c, way in chains:
                advance(c, way, k, j)
            if k == half - 2:
                for c, way in long:
                    hop(c, way, half - 1, j).start()
            due = ((k - 1) * CHUNKS + j + 1) * (farthest - 1) // ((half - 2) * CHUNKS)
            while heard < due:
                heard = listen(heard)
        if k == 1:
            at_old = equal(position, old_place_ref[...]).astype(BF16)
            held_new = dot_nt(at_new, expert_of_slot(new_owner_ref[...], 1)).astype(BF16)
            held_old = dot_nt(at_old, expert_of_slot(old_owner_ref[...], 1)).astype(BF16)
            pairs = dot_nt(held_new, held_old)
            tall_row, tall_column = iota((tall, tall), 0), iota((tall, tall), 1)
            match[...] = jnp.where((tall_row % 4) == (tall_column % 4), pairs, 0.0).astype(BF16)
        if k == 2:
            q, r = tall_row // rows, tall_row % rows
            order[0] = equal(tall_column, (r // 2) * 8 + q * 2 + r % 2).astype(BF16)
            owner = (r % piece) // 2 * CHUNKS + r // piece
            order[1] = equal(tall_column, owner * 8 + q * 2 + r % 2).astype(BF16)
            low = 4 * piece
            low_row, low_column = iota((low, low), 0), iota((low, low), 1)
            q, r = low_column // piece, low_column % piece
            piece_order[...] = equal(low_row, (r // 2) * 8 + q * 2 + r % 2).astype(BF16)

    group = nodes // CHUNKS
    line = group // CHIPS_X
    steps = sorted(
        range(group),
        key=lambda k: -distance((k // line, k % line * CHIPS_Z // line)),
    )
    hosts = [
        (
            k,
            lax.rem(node // (line * CHUNKS) + k // line, CHIPS_X) * line
            + lax.rem(node // CHUNKS + k % line, line),
        )
        for k in steps
    ]
    for j in range(CHUNKS):
        for c in range(2):
            value = parts[slot[(c, 1, 0)], pl.ds(j * piece, piece), :]
            for key in [(c, 1, half - 2), (c, -1, half - 2), (c, 1, half - 1), (c, -1, half - 1)]:
                if key in slot:
                    hop(*key, j).wait_recv()
                    value = value + ring_recv[slot[key], pl.ds(j * piece, piece), :].astype(F32)
            value = value.astype(BF16)
            for h in range(2):
                total[j, pl.ds((2 * c + h) * piece, piece), :] = value[:, h * LANES : (h + 1) * LANES]
        mine = dot(piece_order[...], total[j])
        rows_send[j] = mine.reshape(group, 8, LANES).astype(BF16)

        for step, at in hosts:
            copy = pltpu.make_async_remote_copy(
                src_ref=rows_send.at[j, at],
                dst_ref=rows_recv.at[node],
                send_sem=out_sem.at[1],
                recv_sem=in_sem.at[1],
                device_id=(at * CHUNKS + j, place),
                device_id_type=MESH,
            )
            if step:
                copy.start()
            else:
                pl.when(lax.rem(node, CHUNKS) != j)(copy.start)

    rows_recv[node] = rows_send[lax.rem(node, CHUNKS), node // CHUNKS]

    outs = (out_weight, out_first, out_second, out_grad)

    def natural(block, a):
        value = dot(order[a // 3], block.astype(F32).reshape(tall, LANES).astype(BF16))
        for c in range(2):
            for h in range(2):
                outs[a][c, :, h * LANES : (h + 1) * LANES] = value[
                    (2 * c + h) * rows : (2 * c + h + 1) * rows
                ].astype(BF16)

    all_but_one(state_send, state_recv, 0).wait_recv()
    for a in range(3):
        natural(state_recv[:, a], a)

    all_but_one(rows_recv, rows_recv, 1).wait_recv()
    owned = rows_recv[...].astype(F32).reshape(tall, LANES).astype(BF16)
    stretch = nodes // CHIPS_X
    for dx in sorted(range(CHIPS_X), key=lambda dx: -min(dx, CHIPS_X - dx)):
        to_x = lax.rem(x + dx, CHIPS_X)
        at = pl.multiple_of(to_x * (8 * stretch), 8 * stretch)
        summed = dot(match[pl.ds(at, 8 * stretch), :], owned)
        slots_send[pl.ds(to_x * stretch, stretch)] = summed.reshape(stretch, 8, LANES).astype(BF16)
        scatter(slots_send, slots_recv, 2, [o for o in offsets if o[0] == dx])
    slots_recv[node] = slots_send[node]

    for key, length in chains.items():
        for k in range(length):
            for j in range(CHUNKS):
                hop(*key, k, j).wait_send()
    all_but_one(state_send, state_recv, 0).wait_send()
    all_but_one(rows_recv, rows_recv, 1).wait_send()
    all_but_one(slots_send, slots_recv, 2).wait_recv()
    natural(slots_recv[...], 3)
    all_but_one(slots_send, slots_recv, 2).wait_send()


def by_row(state):
    experts = state.shape[0]
    return state.reshape(experts, 2, 2, LANES).transpose(0, 2, 1, 3).reshape(4 * experts, LANES)


def local(
    master_weight,
    first_moment,
    second_moment,
    features,
    grad_out,
    old_place,
    new_place,
    old_owner,
    new_owner,
):
    nodes, ring = lax.axis_size("node"), lax.axis_size("local")
    experts = master_weight.shape[0]
    rows = features.shape[3]
    columns = master_weight.shape[2]
    tall = 8 * nodes
    hops = 2 * (ring - 1)
    piece = rows // CHUNKS
    operands = (
        old_place.reshape(1, -1),
        new_place.reshape(1, -1),
        old_owner.reshape(1, -1),
        new_owner.reshape(1, -1),
        by_row(master_weight),
        by_row(first_moment),
        by_row(second_moment),
        features.reshape(2, features.shape[2], rows),
        grad_out.reshape(2, grad_out.shape[2], grad_out.shape[3]),
    )
    hbm = pl.BlockSpec(memory_space=pltpu.HBM)
    operands = tuple(pltpu.with_memory_space_constraint(x, pltpu.HBM) for x in operands)
    block = pltpu.VMEM((2, rows, columns), BF16)
    weight_old, first_old, second_old, gradient = pl.pallas_call(
        functools.partial(exchange, nodes, ring),
        out_shape=(block,) * 4,
        in_specs=[hbm] * len(operands),
        out_specs=(pl.BlockSpec(memory_space=pltpu.VMEM),) * 4,
        scratch_shapes=[
            *(pltpu.VMEM(operand.shape, operand.dtype) for operand in operands),
            pltpu.SemaphoreType.DMA((len(operands),)),
            pltpu.SemaphoreType.DMA((hops + 2,)),
            pltpu.VMEM((2, rows, features.shape[2]), BF16),
            pltpu.VMEM((hops, rows, columns), BF16),
            pltpu.VMEM((hops, rows, columns), BF16),
            pltpu.VMEM((nodes, 3, 8, LANES), BF16),
            pltpu.VMEM((nodes, 3, 8, LANES), BF16),
            pltpu.VMEM((CHUNKS, nodes // CHUNKS, 8, LANES), BF16),
            pltpu.VMEM((nodes, 8, LANES), BF16),
            pltpu.VMEM((nodes, 8, LANES), BF16),
            pltpu.VMEM((nodes, 8, LANES), BF16),
            pltpu.VMEM((hops, rows, columns), F32),
            pltpu.VMEM((CHUNKS, 4 * piece, LANES), BF16),
            pltpu.VMEM((4 * piece, 4 * piece), BF16),
            pltpu.VMEM((2, tall, tall), BF16),
            pltpu.VMEM((tall, tall), BF16),
            pltpu.SemaphoreType.DMA((hops, CHUNKS)),
            pltpu.SemaphoreType.DMA((hops, CHUNKS)),
            pltpu.SemaphoreType.DMA((3,)),
            pltpu.SemaphoreType.DMA((3,)),
            pltpu.SemaphoreType.REGULAR((CHIPS_X // 2 + CHIPS_Z // 2 - 1,)),
        ],
        compiler_params=pltpu.CompilerParams(
            collective_id=0, has_side_effects=True, vmem_limit_bytes=40 * 1024 * 1024
        ),
        name="exchange",
    )(*operands)
    gradient = gradient.astype(F32)
    first_new = BETA_FIRST * first_old.astype(F32) + (1.0 - BETA_FIRST) * gradient
    second_new = BETA_SECOND * second_old.astype(F32) + (1.0 - BETA_SECOND) * gradient * gradient
    weight_old = weight_old.astype(F32)
    update = (
        first_new / CORRECT_FIRST / (jnp.sqrt(second_new / CORRECT_SECOND) + EPSILON)
        + DECAY_RATE * weight_old
    )
    weight_new = (weight_old - LEARNING_RATE * update).astype(BF16)
    return weight_new, first_new, second_new


def solution(mesh):
    return jax.shard_map(
        local,
        mesh=mesh,
        in_specs=(
            P(None, "node", "local"),
            P(None, "node", "local"),
            P(None, "node", "local"),
            P("node", "local", None, None),
            P("node", "local", None, None),
            P(),
            P(),
            P(),
            P(),
        ),
        out_specs=(P("node", None, "local"), P("node", None, "local"), P("node", None, "local")),
        check_vma=False,
    )
```

```python
import functools

import jax
import jax.numpy as jnp
from jax import lax
from jax.experimental import pallas as pl
from jax.experimental.pallas import tpu as pltpu
from jax.sharding import PartitionSpec as P

BETA_FIRST = 0.9
BETA_SECOND = 0.95
LEARNING_RATE = 0.1
DECAY_RATE = 0.1
EPSILON = 1e-08
CORRECT_FIRST = 1.0 - 0.9**10
CORRECT_SECOND = 1.0 - 0.95**10

MESH = pl.DeviceIdType.MESH
LANES = 128
CHUNKS = 2
CHIPS_X, CHIPS_Z = 4, 8
F32 = jnp.float32
BF16 = jnp.bfloat16


def dot(a, b):
    return jnp.dot(a, b, preferred_element_type=F32)


def dot_nt(a, b):
    return lax.dot_general(a, b, (((1,), (1,)), ((), ())), preferred_element_type=F32)


def equal(a, b):
    return jnp.where(a == b, 1.0, 0.0)


def iota(shape, axis):
    return lax.broadcasted_iota(jnp.int32, shape, axis)


def exchange(
    nodes,
    ring,
    old_place_hbm,
    new_place_hbm,
    old_owner_hbm,
    new_owner_hbm,
    weight_hbm,
    first_hbm,
    second_hbm,
    features_hbm,
    grad_hbm,
    out_weight,
    out_first,
    out_second,
    out_grad,
    old_place_ref,
    new_place_ref,
    old_owner_ref,
    new_owner_ref,
    weight_ref,
    first_ref,
    second_ref,
    features_ref,
    grad_ref,
    load_sem,
    block_sem,
    turned,
    ring_send,
    ring_recv,
    state_send,
    state_recv,
    rows_send,
    rows_recv,
    slots_send,
    slots_recv,
    parts,
    total,
    piece_order,
    order,
    match,
    ring_out_sem,
    ring_in_sem,
    out_sem,
    in_sem,
    round_sem,
):
    node = lax.axis_index("node")
    place = lax.axis_index("local")
    experts = weight_ref.shape[0] // 4
    rows = features_ref.shape[2]
    columns = 2 * LANES
    tall = 8 * nodes
    half = ring // 2
    loads = [
        pltpu.make_async_copy(source, target, load_sem.at[i])
        for i, (source, target) in enumerate(
            (
                (features_hbm, features_ref),
                (new_place_hbm, new_place_ref),
                (new_owner_hbm, new_owner_ref),
                (weight_hbm, weight_ref),
                (first_hbm, first_ref),
                (second_hbm, second_ref),
                (old_place_hbm, old_place_ref),
                (old_owner_hbm, old_owner_ref),
            )
        )
    ]

    x, z, core = node // (2 * CHIPS_Z), lax.rem(node // 2, CHIPS_Z), lax.rem(node, 2)

    def away(dx, dz, dc):
        to_x = lax.rem(x + dx, CHIPS_X) if dx else x
        to_z = lax.rem(z + dz, CHIPS_Z) if dz else z
        return (to_x * CHIPS_Z + to_z) * 2 + (1 - core if dc else core)

    def distance(offset):
        dx, dz = offset[0], offset[1]
        return min(dx, CHIPS_X - dx) + min(dz, CHIPS_Z - dz)

    offsets = [(dx, dz, dc) for dx in range(CHIPS_X) for dz in range(CHIPS_Z) for dc in range(2)][1:]
    offsets.sort(key=distance, reverse=True)
    farthest = distance(offsets[0])
    next_to = [(1, 0), (CHIPS_X - 1, 0), (0, 1), (0, CHIPS_Z - 1)]

    barrier = pltpu.get_barrier_semaphore()
    right = lax.rem(place + 1, ring)
    left = lax.rem(place + ring - 1, ring)
    right_two = lax.rem(place + 2, ring)
    left_two = lax.rem(place + ring - 2, ring)
    for neighbour in (right, left, right_two, left_two):
        pl.semaphore_signal(barrier, inc=1, device_id=(node, neighbour), device_id_type=MESH)
    close = [(0, 0, 1)] + [(dx, dz, dc) for dx, dz in next_to for dc in range(2)]
    for offset in close:
        pl.semaphore_signal(barrier, inc=1, device_id=(away(*offset), place), device_id_type=MESH)

    def tell(r):
        for dx, dz in next_to:
            pl.semaphore_signal(
                round_sem.at[r - 1], inc=1, device_id=(away(dx, dz, 0), place), device_id_type=MESH
            )

    def hear(r):
        pl.semaphore_wait(round_sem.at[r - 1], len(next_to))

    chains = {(0, 1): half, (1, -1): half, (0, -1): half - 1, (1, 1): half - 1}
    slot = {}
    for k in range(half):
        for key, length in chains.items():
            if k < length:
                slot[key + (k,)] = len(slot)
    long = [key for key in chains if chains[key] == half]
    short = [key for key in chains if chains[key] < half]
    piece = rows // CHUNKS

    def columns_ahead(ahead):
        block = lax.rem(place + ahead + ring, ring)
        return pl.ds(pl.multiple_of(block * columns, columns), columns)

    needs = [(c, way * (chains[(c, way)] - k)) for c, way, k in slot] + [(0, 0), (1, 0)]
    blocks = {}
    for i, (c, ahead) in enumerate(needs):
        at = columns_ahead(ahead)
        blocks[(c, ahead)] = pltpu.make_async_copy(
            grad_hbm.at[c, :, at], grad_ref.at[c, :, at], block_sem.at[i]
        )
    loads[0].start()
    for need in needs[: len(chains)]:
        blocks[need].start()
    for load in loads[1:]:
        load.start()
    for need in needs[len(chains) :]:
        blocks[need].start()
    loads[0].wait()
    for c in range(2):
        turned[c] = features_ref[c].astype(F32).T.astype(BF16)

    def partial(c, ahead):
        blocks[(c, ahead)].wait()
        return dot(turned[c], grad_ref[c, :, columns_ahead(ahead)])

    def hop(c, way, k, j=0):
        at = slot[(c, way, k)]
        if (c, way) in long and k == half - 2:
            to = right_two if way == 1 else left_two
        else:
            to = right if way == 1 else left
        some = pl.ds(j * piece, piece)
        return pltpu.make_async_remote_copy(
            src_ref=ring_send.at[at, some],
            dst_ref=ring_recv.at[at, some],
            send_sem=ring_out_sem.at[at, j],
            recv_sem=ring_in_sem.at[at, j],
            device_id=(node, to),
            device_id_type=MESH,
        )

    def advance(c, way, k, j):
        at, before, some = slot[(c, way, k)], slot[(c, way, k - 1)], pl.ds(j * piece, piece)
        hop(c, way, k - 1, j).wait_recv()
        ring_send[at, some] = (parts[at, some] + ring_recv[before, some].astype(F32)).astype(BF16)
        hop(c, way, k, j).start()

    for c, way in chains:
        ring_send[slot[(c, way, 0)]] = partial(c, way * chains[(c, way)]).astype(BF16)
    pl.semaphore_wait(barrier, 4 + len(close))
    for j in range(CHUNKS):
        for c, way in chains:
            hop(c, way, 0, j).start()
    tell(1)
    for (c, way, k), at in slot.items():
        if k == half - 1:
            ring_send[at] = partial(c, way).astype(BF16)
        elif k:
            parts[at] = partial(c, way * (chains[(c, way)] - k))
    for c in range(2):
        parts[slot[(c, 1, 0)]] = partial(c, 0)

    def scatter(send, recv, which, some):
        for offset in some:
            other = away(*offset)
            pltpu.make_async_remote_copy(
                src_ref=send.at[other],
                dst_ref=recv.at[node],
                send_sem=out_sem.at[which],
                recv_sem=in_sem.at[which],
                device_id=(other, place),
                device_id_type=MESH,
            ).start()

    def state_up_to(low, high):
        scatter(state_send, state_recv, 0, [o for o in offsets if low <= distance(o) <= high])

    def all_but_one(send, recv, which):
        return pltpu.make_async_remote_copy(
            src_ref=send.at[pl.ds(0, nodes - 1)],
            dst_ref=recv.at[pl.ds(0, nodes - 1)],
            send_sem=out_sem.at[which],
            recv_sem=in_sem.at[which],
            device_id=(lax.rem(node + 1, nodes), place),
            device_id_type=MESH,
        )

    for load in loads[1:]:
        load.wait()
    redundant = old_owner_ref.shape[1]
    slots = experts + redundant
    position = iota((tall, slots), 0) // 4

    def expert_of_slot(owner, repeat):
        owned = equal(iota((experts * repeat, redundant), 0) // repeat, owner).astype(BF16)
        tail = equal(iota((redundant, slots), 0) + experts, iota((redundant, slots), 1)).astype(BF16)
        primary = equal(iota((experts * repeat, slots), 0) // repeat, iota((experts * repeat, slots), 1))
        return (dot(owned, tail) + primary).astype(BF16)

    at_new = equal(position, new_place_ref[...]).astype(BF16)
    choose = dot_nt(at_new, expert_of_slot(new_owner_ref[...], 4))
    same = (iota((tall, 4 * experts), 0) % 4) == (iota((tall, 4 * experts), 1) % 4)
    choose = jnp.where(same, choose, 0.0).astype(BF16)
    for a, ref in enumerate((weight_ref, first_ref, second_ref)):
        picked = dot(choose, ref[...].astype(BF16))
        state_send[:, a] = picked.reshape(nodes, 8, LANES).astype(BF16)
    state_recv[node] = state_send[node]
    state_up_to(0, 1)
    heard = 0

    def listen(heard):
        if heard == farthest - 1:
            return heard
        heard += 1
        hear(heard)
        if heard < farthest - 1:
            tell(heard + 1)
        state_up_to(heard + 1, heard + 1)
        return heard

    heard = listen(heard)
    for k in range(1, half - 1):
        for j in range(CHUNKS):
            for c, way in chains:
                advance(c, way, k, j)
            if k == half - 2:
                for c, way in long:
                    hop(c, way, half - 1, j).start()
            due = min(farthest - 1, 1 + ((k - 1) * CHUNKS + j + 1) * (farthest - 1) // ((half - 2) * CHUNKS))
            while heard < due:
                heard = listen(heard)
        if k == 1:
            at_old = equal(position, old_place_ref[...]).astype(BF16)
            held_new = dot_nt(at_new, expert_of_slot(new_owner_ref[...], 1)).astype(BF16)
            held_old = dot_nt(at_old, expert_of_slot(old_owner_ref[...], 1)).astype(BF16)
            pairs = dot_nt(held_new, held_old)
            tall_row, tall_column = iota((tall, tall), 0), iota((tall, tall), 1)
            match[...] = jnp.where((tall_row % 4) == (tall_column % 4), pairs, 0.0).astype(BF16)
        if k == 2:
            q, r = tall_row // rows, tall_row % rows
            order[0] = equal(tall_column, (r // 2) * 8 + q * 2 + r % 2).astype(BF16)
            owner = (r % piece) // 2 * CHUNKS + r // piece
            order[1] = equal(tall_column, owner * 8 + q * 2 + r % 2).astype(BF16)
            low = 4 * piece
            low_row, low_column = iota((low, low), 0), iota((low, low), 1)
            q, r = low_column // piece, low_column % piece
            piece_order[...] = equal(low_row, (r // 2) * 8 + q * 2 + r % 2).astype(BF16)

    group = nodes // CHUNKS
    line = group // CHIPS_X
    steps = sorted(
        range(group),
        key=lambda k: -distance((k // line, k % line * CHIPS_Z // line)),
    )
    hosts = [
        (
            k,
            lax.rem(node // (line * CHUNKS) + k // line, CHIPS_X) * line
            + lax.rem(node // CHUNKS + k % line, line),
        )
        for k in steps
    ]
    for j in range(CHUNKS):
        for c in range(2):
            value = parts[slot[(c, 1, 0)], pl.ds(j * piece, piece), :]
            for key in [(c, 1, half - 2), (c, -1, half - 2), (c, 1, half - 1), (c, -1, half - 1)]:
                if key in slot:
                    hop(*key, j).wait_recv()
                    value = value + ring_recv[slot[key], pl.ds(j * piece, piece), :].astype(F32)
            value = value.astype(BF16)
            for h in range(2):
                total[j, pl.ds((2 * c + h) * piece, piece), :] = value[:, h * LANES : (h + 1) * LANES]
        mine = dot(piece_order[...], total[j])
        rows_send[j] = mine.reshape(group, 8, LANES).astype(BF16)

        for step, at in hosts:
            copy = pltpu.make_async_remote_copy(
                src_ref=rows_send.at[j, at],
                dst_ref=rows_recv.at[node],
                send_sem=out_sem.at[1],
                recv_sem=in_sem.at[1],
                device_id=(at * CHUNKS + j, place),
                device_id_type=MESH,
            )
            if step:
                copy.start()
            else:
                pl.when(lax.rem(node, CHUNKS) != j)(copy.start)

    rows_recv[node] = rows_send[lax.rem(node, CHUNKS), node // CHUNKS]

    outs = (out_weight, out_first, out_second, out_grad)

    def natural(block, a):
        value = dot(order[a // 3], block.astype(F32).reshape(tall, LANES).astype(BF16))
        for c in range(2):
            for h in range(2):
                outs[a][c, :, h * LANES : (h + 1) * LANES] = value[
                    (2 * c + h) * rows : (2 * c + h + 1) * rows
                ].astype(BF16)

    all_but_one(state_send, state_recv, 0).wait_recv()
    for a in range(3):
        natural(state_recv[:, a], a)

    all_but_one(rows_recv, rows_recv, 1).wait_recv()
    owned = rows_recv[...].astype(F32).reshape(tall, LANES).astype(BF16)
    stretch = nodes // CHIPS_X
    for dx in sorted(range(CHIPS_X), key=lambda dx: -min(dx, CHIPS_X - dx)):
        to_x = lax.rem(x + dx, CHIPS_X)
        at = pl.multiple_of(to_x * (8 * stretch), 8 * stretch)
        summed = dot(match[pl.ds(at, 8 * stretch), :], owned)
        slots_send[pl.ds(to_x * stretch, stretch)] = summed.reshape(stretch, 8, LANES).astype(BF16)
        scatter(slots_send, slots_recv, 2, [o for o in offsets if o[0] == dx])
    slots_recv[node] = slots_send[node]

    for key, length in chains.items():
        for k in range(length):
            for j in range(CHUNKS):
                hop(*key, k, j).wait_send()
    all_but_one(state_send, state_recv, 0).wait_send()
    all_but_one(rows_recv, rows_recv, 1).wait_send()
    all_but_one(slots_send, slots_recv, 2).wait_recv()
    natural(slots_recv[...], 3)
    all_but_one(slots_send, slots_recv, 2).wait_send()


def by_row(state):
    experts = state.shape[0]
    return state.reshape(experts, 2, 2, LANES).transpose(0, 2, 1, 3).reshape(4 * experts, LANES)


def local(
    master_weight,
    first_moment,
    second_moment,
    features,
    grad_out,
    old_place,
    new_place,
    old_owner,
    new_owner,
):
    nodes, ring = lax.axis_size("node"), lax.axis_size("local")
    experts = master_weight.shape[0]
    rows = features.shape[3]
    columns = master_weight.shape[2]
    tall = 8 * nodes
    hops = 2 * (ring - 1)
    piece = rows // CHUNKS
    operands = (
        old_place.reshape(1, -1),
        new_place.reshape(1, -1),
        old_owner.reshape(1, -1),
        new_owner.reshape(1, -1),
        by_row(master_weight),
        by_row(first_moment),
        by_row(second_moment),
        features.reshape(2, features.shape[2], rows),
        grad_out.reshape(2, grad_out.shape[2], grad_out.shape[3]),
    )
    hbm = pl.BlockSpec(memory_space=pltpu.HBM)
    operands = tuple(pltpu.with_memory_space_constraint(x, pltpu.HBM) for x in operands)
    block = pltpu.VMEM((2, rows, columns), BF16)
    weight_old, first_old, second_old, gradient = pl.pallas_call(
        functools.partial(exchange, nodes, ring),
        out_shape=(block,) * 4,
        in_specs=[hbm] * len(operands),
        out_specs=(pl.BlockSpec(memory_space=pltpu.VMEM),) * 4,
        scratch_shapes=[
            *(pltpu.VMEM(operand.shape, operand.dtype) for operand in operands),
            pltpu.SemaphoreType.DMA((len(operands),)),
            pltpu.SemaphoreType.DMA((hops + 2,)),
            pltpu.VMEM((2, rows, features.shape[2]), BF16),
            pltpu.VMEM((hops, rows, columns), BF16),
            pltpu.VMEM((hops, rows, columns), BF16),
            pltpu.VMEM((nodes, 3, 8, LANES), BF16),
            pltpu.VMEM((nodes, 3, 8, LANES), BF16),
            pltpu.VMEM((CHUNKS, nodes // CHUNKS, 8, LANES), BF16),
            pltpu.VMEM((nodes, 8, LANES), BF16),
            pltpu.VMEM((nodes, 8, LANES), BF16),
            pltpu.VMEM((nodes, 8, LANES), BF16),
            pltpu.VMEM((hops, rows, columns), F32),
            pltpu.VMEM((CHUNKS, 4 * piece, LANES), BF16),
            pltpu.VMEM((4 * piece, 4 * piece), BF16),
            pltpu.VMEM((2, tall, tall), BF16),
            pltpu.VMEM((tall, tall), BF16),
            pltpu.SemaphoreType.DMA((hops, CHUNKS)),
            pltpu.SemaphoreType.DMA((hops, CHUNKS)),
            pltpu.SemaphoreType.DMA((3,)),
            pltpu.SemaphoreType.DMA((3,)),
            pltpu.SemaphoreType.REGULAR((CHIPS_X // 2 + CHIPS_Z // 2 - 1,)),
        ],
        compiler_params=pltpu.CompilerParams(
            collective_id=0, has_side_effects=True, vmem_limit_bytes=40 * 1024 * 1024
        ),
        name="exchange",
    )(*operands)
    gradient = gradient.astype(F32)
    first_new = BETA_FIRST * first_old.astype(F32) + (1.0 - BETA_FIRST) * gradient
    second_new = BETA_SECOND * second_old.astype(F32) + (1.0 - BETA_SECOND) * gradient * gradient
    weight_old = weight_old.astype(F32)
    update = (
        first_new / CORRECT_FIRST / (jnp.sqrt(second_new / CORRECT_SECOND) + EPSILON)
        + DECAY_RATE * weight_old
    )
    weight_new = (weight_old - LEARNING_RATE * update).astype(BF16)
    return weight_new, first_new, second_new


def solution(mesh):
    return jax.shard_map(
        local,
        mesh=mesh,
        in_specs=(
            P(None, "node", "local"),
            P(None, "node", "local"),
            P(None, "node", "local"),
            P("node", "local", None, None),
            P("node", "local", None, None),
            P(),
            P(),
            P(),
            P(),
        ),
        out_specs=(P("node", None, "local"), P("node", None, "local"), P("node", None, "local")),
        check_vma=False,
    )
```
